32 devices in a mesh: grp: 4 (over y, core), cls: 8 (over z, x).
Axes of the slice: x: 2, y: 2, z: 4, core: 2. Of those that a mesh axis runs over, the one named last changes fastest.
Arguments:
- particles: float32 [1024, 128, 128], P(('grp', 'cls')), may hold values from -6 to 6
- references: float32 [256, 2, 128, 128], P('cls'), may hold values from -6 to 6
- class_of: int32 [1024], P(('grp', 'cls')), may hold values from 0 to 255, as said below
- rotation_bin: int32 [1024], P(('grp', 'cls')), may hold values from 0 to 3
- shift_best: int32 [1024], P(('grp', 'cls')), may hold values from 0 to 63
- defocus_bin: int32 [1024], P(('grp', 'cls')), may hold values from 0 to 15
- shift_list: int32 [64, 2], replicated, may hold values from -8 to 8
- defocus: float32 [16], replicated, may hold values from 8 to 64
Outputs:
- scores: float32 [1024, 64], P(('grp', 'cls'))
- new_references: float32 [256, 2, 128, 128], P(('cls', 'grp'))
The draws below stay inside these ranges and needn't reach their ends.
Inputs may be any that keep to these rules, and one draw needn't show every extreme that they name: `class_of`: class c belongs to owner c // 32. Among the 32 particles of one device (aligned blocks of 32 rows), at most 8 belong to the classes of one owner, and in every draw one owner holds exactly 8 from every device.
All inputs are finite; a program needn't handle non-finite values.
Results may differ from the reference program's by a relative error of at most 0.0003.
Values sent between devices are 32-bit elements; how exact they have to be, the bound alone decides.
A program may use at most 128 MiB of HBM per device.

```python
import math
import jax
import jax.numpy as jnp
from jax import lax

IMG = 128
NSHIFT = 64
NDEF = 16
CLS_DEV = 32
PART_DEV = 32
CLASSES = 256
PARTICLES = 1024
CAP = 8
N_GRP = 4
N_CLS = 8


def draw_class_of(key, part):
    key = jax.random.fold_in(key, 7)
    key_level, key_heavy, key_noise, key_order, key_local = jax.random.split(key, 5)
    slot_total = N_CLS * CAP
    blocks = N_GRP * N_CLS
    slot_owner = jnp.arange(slot_total, dtype=jnp.int32) // CAP
    busy_level = jax.random.randint(key_level, (N_CLS,), 0, 4)
    heavy_owner = jax.random.randint(key_heavy, (), 0, N_CLS)
    noise_draw = jax.random.randint(key_noise, (blocks, slot_total), 0, 4096)
    priority = noise_draw + busy_level[slot_owner] * 2048 + jnp.where(slot_owner == heavy_owner, 65536, 0)
    priority = priority * slot_total + jnp.arange(slot_total, dtype=jnp.int32)
    picked = lax.top_k(priority, PART_DEV)[1]
    owners = slot_owner[picked]
    shuffle_keys = jax.random.randint(key_order, (blocks, PART_DEV), 0, 65536) * PART_DEV + jnp.arange(PART_DEV, dtype=jnp.int32)
    shuffle_order = jnp.argsort(shuffle_keys, axis=1, stable=True)
    owners = jnp.take_along_axis(owners, shuffle_order, axis=1)
    local_class = jax.random.randint(key_local, (blocks, PART_DEV), 0, CLS_DEV)
    return (owners * CLS_DEV + local_class).reshape(blocks * PART_DEV).astype(jnp.int32)


def plant(result, stream_key, least, largest):
    extent = result.shape
    index_at = [jax.random.randint(jax.random.fold_in(stream_key, axis), (), 0, extent[axis]) for axis in range(len(extent))]
    result = result.at[tuple(index_at)].set(least)
    longest = extent.index(max(extent))
    index_at[longest] = (index_at[longest] + 1) % extent[longest]
    return result.at[tuple(index_at)].set(largest)


def steps_of(stream_key, shape, cuts, smallest, top_value):
    gain = 1.0
    for axis_at, blocks in cuts:
        draws = jax.random.uniform(jax.random.fold_in(jax.random.fold_in(stream_key, 6), axis_at), (blocks,), jnp.float32, smallest / len(cuts), top_value / len(cuts))
        gain = gain * jnp.repeat(jnp.exp(draws), shape[axis_at] // blocks).reshape((-1,) + (1,) * (len(shape) - 1 - axis_at))
    return gain


def normal_values(rng, dims, scale, most, cuts=(), kind=jnp.bfloat16):
    gain = steps_of(rng, dims, cuts, -0.22, 0.18) if cuts else 1.0
    drawn = jax.random.normal(rng, dims, jnp.float32) * scale * gain
    return jnp.minimum(jnp.maximum(drawn, -most), most).astype(kind)


def setup_inputs(seed: int = 0) -> dict:
    arg_keys = jax.random.split(jax.random.key(seed), 9)
    return {
        "particles": normal_values(arg_keys[0], (PARTICLES, IMG, IMG), 1.0, 6.0, ((0, 32),), jnp.float32),
        "references": normal_values(arg_keys[1], (CLASSES, 2, IMG, IMG), 1.0, 6.0, ((0, 8),), jnp.float32),
        "class_of": draw_class_of(jax.random.fold_in(arg_keys[8], 71), 0),
        "rotation_bin": plant(jax.random.randint(arg_keys[3], (PARTICLES,), 0, 4), jax.random.fold_in(arg_keys[3], 1), 0, 3).astype(jnp.int32),
        "shift_best": plant(jax.random.randint(arg_keys[4], (PARTICLES,), 0, NSHIFT), jax.random.fold_in(arg_keys[4], 1), 0, NSHIFT - 1).astype(jnp.int32),
        "defocus_bin": plant(jax.random.randint(arg_keys[5], (PARTICLES,), 0, NDEF), jax.random.fold_in(arg_keys[5], 1), 0, NDEF - 1).astype(jnp.int32),
        "shift_list": plant(jax.random.randint(arg_keys[6], (NSHIFT, 2), -8, 9), jax.random.fold_in(arg_keys[6], 1), -8, 8).astype(jnp.int32),
        "defocus": jnp.clip(jnp.exp(jax.random.uniform(arg_keys[7], (NDEF,), jnp.float32, math.log(8.0), math.log(64.0))), 8.0, 64.0),
    }


highest = lax.Precision.HIGHEST

def dft_tables(image_side):
    pixel_index = jnp.arange(image_side, dtype=jnp.int32)
    turn_grid = (pixel_index[:, None] * pixel_index[None, :] % image_side).astype(jnp.float32)
    angles = turn_grid * (2.0 * math.pi / image_side)
    norm_scale = 1.0 / math.sqrt(image_side)
    cos_table = jnp.cos(angles) * norm_scale
    sin_table = jnp.sin(angles) * norm_scale
    right_table = jnp.concatenate([cos_table, sin_table], axis=1)
    left_table = jnp.stack([jnp.stack([cos_table, -sin_table], axis=1), jnp.stack([-sin_table, -cos_table], axis=1)], axis=0)
    return (right_table, left_table)

def spectra(images, right_table, left_table):
    image_side = images.shape[-1]
    halfway = jnp.einsum('...jk,kl->...jl', images, right_table, precision=highest)
    halfway = halfway.reshape(halfway.shape[:-1] + (2, image_side))
    return jnp.einsum('aibj,...jbl->...ail', left_table, halfway, precision=highest)

def rotate(images, quarter_turns):
    turn_grid = quarter_turns[:, None, None]
    rot_one = jnp.rot90(images, 1, axes=(1, 2))
    rot_two = jnp.rot90(images, 2, axes=(1, 2))
    rot_three = jnp.rot90(images, 3, axes=(1, 2))
    return jnp.where(turn_grid == 0, images, jnp.where(turn_grid == 1, rot_one, jnp.where(turn_grid == 2, rot_two, rot_three)))

def contrast_table(defocus, image_side):
    pixel_index = jnp.arange(image_side, dtype=jnp.int32)
    signed = jnp.where(pixel_index < image_side // 2, pixel_index, pixel_index - image_side).astype(jnp.float32)
    radius = (signed[:, None] * signed[:, None] + signed[None, :] * signed[None, :]) / float((image_side // 2) ** 2)
    phases = defocus[:, None, None] * radius[None, :, :]
    return -(0.995 * jnp.sin(phases) + 0.1 * jnp.cos(phases))

def shift_tables(shift_list, image_side):
    pixel_index = jnp.arange(image_side, dtype=jnp.int32)
    turn_grid = (pixel_index[None, :, None] * shift_list[:, 0][:, None, None] + pixel_index[None, None, :] * shift_list[:, 1][:, None, None]) % image_side
    angles = turn_grid.astype(jnp.float32) * (2.0 * math.pi / image_side)
    return (jnp.cos(angles), jnp.sin(angles))

def make_score_table(shift_cos, shift_sin):
    shift_count = shift_cos.shape[0]
    return jnp.concatenate([shift_cos.reshape(shift_count, -1).T, -shift_sin.reshape(shift_count, -1).T], axis=0)

def particle_terms(spectrum, ref_rows, contrast, best_cos, best_sin, score_table, image_side):
    sign_pair = jnp.array([1.0, -1.0], jnp.float32)[None, :, None, None]
    swapped = spectrum[:, ::-1]
    ref_real = ref_rows[:, 0][:, None]
    ref_imag = ref_rows[:, 1][:, None]
    contrast_pair = contrast[:, None]
    product = contrast_pair * (spectrum * ref_real + swapped * ref_imag * sign_pair)
    item_count = spectrum.shape[0]
    scores = jnp.dot(product.reshape(item_count, -1), score_table, precision=highest, preferred_element_type=jnp.float32) / image_side
    contrib = contrast_pair * (spectrum * best_cos[:, None] - swapped * best_sin[:, None] * sign_pair)
    return (scores, contrib, contrast * contrast)

def reference(particles, references, class_of, rotation_bin, shift_best, defocus_bin, shift_list, defocus):
    image_side = particles.shape[-1]
    right_table, left_table = dft_tables(image_side)
    shift_cos, shift_sin = shift_tables(shift_list, image_side)
    score_table = make_score_table(shift_cos, shift_sin)
    block_rows = math.gcd(PARTICLES, 512)
    block_count = PARTICLES // block_rows

    def accumulate(running, block_start):
        numerator, weight_sum = running
        block_images = lax.dynamic_slice_in_dim(particles, block_start, block_rows, 0)
        block_class = lax.dynamic_slice_in_dim(class_of, block_start, block_rows, 0)
        block_turns = lax.dynamic_slice_in_dim(rotation_bin, block_start, block_rows, 0)
        block_best = lax.dynamic_slice_in_dim(shift_best, block_start, block_rows, 0)
        block_bins = lax.dynamic_slice_in_dim(defocus_bin, block_start, block_rows, 0)
        spectrum = spectra(rotate(block_images, block_turns), right_table, left_table)
        best_cos, best_sin = shift_tables(shift_list[block_best], image_side)
        contrast = contrast_table(defocus[block_bins], image_side)
        scores, contrib, weight = particle_terms(spectrum, references[block_class], contrast, best_cos, best_sin, score_table, image_side)
        numerator = numerator.at[block_class].add(contrib)
        weight_sum = weight_sum.at[block_class].add(weight)
        return ((numerator, weight_sum), scores)
    starts = jnp.arange(block_count, dtype=jnp.int32) * block_rows
    initial = (jnp.zeros((CLASSES, 2, image_side, image_side), jnp.float32), jnp.zeros((CLASSES, image_side, image_side), jnp.float32))
    (numerator, weight_sum), scores = lax.scan(accumulate, initial, starts)
    fresh_refs = numerator / (weight_sum[:, None] + 1.0)
    return (scores.reshape(PARTICLES, NSHIFT), fresh_refs)
```

```python
import functools
import math

import jax
import jax.numpy as jnp
from jax import lax
from jax.experimental import pallas as pl
from jax.experimental.pallas import tpu as pltpu
from jax.sharding import PartitionSpec as P

f32, bf16 = jnp.float32, jnp.bfloat16
HALF = 72
GROUP = 8
VMEM_BYTES = 56 * 1024 * 1024


def split(x):
    high = x.astype(bf16)
    return high, (x - high.astype(f32)).astype(bf16)


def split_table(x):
    high = lax.reduce_precision(x, 8, 7)
    return high.astype(bf16), lax.reduce_precision(x - high, 8, 7).astype(bf16)


def dot(a, b):
    return jnp.dot(a, b, preferred_element_type=f32)


def dot3(a, b):
    return dot(a[0], b[0]) + (dot(a[1], b[0]) + dot(a[0], b[1]))


def circle(turns, side):
    angles = (turns % side).astype(f32) * (2.0 * math.pi / side)
    return jnp.cos(angles), jnp.sin(angles)


def dft_tables(side):
    pixel = jnp.arange(side, dtype=jnp.int32)
    norm = 1.0 / math.sqrt(side)
    cos_table, sin_table = circle(pixel[:, None] * pixel[None, :], side)
    cos_table, sin_table = cos_table * norm, sin_table * norm
    flip_cos, flip_sin = circle(pixel[:, None] * (side - 1 - pixel)[None, :], side)
    flip_cos, flip_sin = flip_cos * norm, flip_sin * norm
    right = jnp.stack(
        [
            jnp.concatenate([cos_table, sin_table], axis=1),
            jnp.concatenate([flip_cos.T, flip_sin.T], axis=1),
        ]
    )
    live = (jnp.arange(HALF) <= side // 2)[:, None].astype(f32)

    def left(c, s):
        c, s = c[:HALF] * live, s[:HALF] * live
        return jnp.concatenate(
            [jnp.concatenate([c, -s], axis=1), jnp.concatenate([-s, -c], axis=1)], axis=0
        )

    return right, jnp.stack([left(cos_table, sin_table), left(flip_cos, flip_sin)])


def contrast_half(defocus, side):
    pixel = jnp.arange(side, dtype=jnp.int32)
    signed = jnp.where(pixel < side // 2, pixel, pixel - side).astype(f32)
    rows = signed[:HALF]
    radius = (rows[:, None] * rows[:, None] + signed[None, :] * signed[None, :]) / float(
        (side // 2) ** 2
    )
    phases = defocus[:, None, None] * radius[None]
    return -(0.995 * jnp.sin(phases) + 0.1 * jnp.cos(phases))


def shift_tables(shift_list, side):
    row_cos, row_sin = circle(
        shift_list[:, 0][:, None] * jnp.arange(HALF, dtype=jnp.int32)[None, :], side
    )
    col_cos, col_sin = circle(
        shift_list[:, 1][:, None] * jnp.arange(side, dtype=jnp.int32)[None, :], side
    )
    rc, rs = row_cos[:, :, None], row_sin[:, :, None]
    cc, cs = col_cos[:, None, :], col_sin[:, None, :]
    phase = jnp.stack([rc * cc - rs * cs, rs * cc + rc * cs], axis=1)
    score_right = jnp.concatenate([col_cos.T, col_sin.T], axis=1)
    row = jnp.arange(HALF)
    times = jnp.where(
        (row == 0) | (row == side // 2), 1.0, jnp.where(row < side // 2, 2.0, 0.0)
    ).astype(f32)[:, None] / side
    uc, us = row_cos.T * times, row_sin.T * times
    score_left = jnp.concatenate(
        [jnp.concatenate([uc, -us], axis=1), jnp.concatenate([-us, -uc], axis=1)], axis=0
    )
    return phase, score_right, score_left


def mirror_pick(rows, cols, side, offset):
    i = lax.broadcasted_iota(jnp.int32, (rows, cols), 0)
    j = lax.broadcasted_iota(jnp.int32, (rows, cols), 1)
    return jnp.where((i + j) % side == offset, 1.0, 0.0).astype(bf16)


def mirrored(x, row_pick, col_pick):
    total = None
    for piece in split(x):
        turned = dot(dot(row_pick, piece).astype(bf16), col_pick)
        total = turned if total is None else total + turned
    return total


def reference_half_kernel(side, ref, out):
    row_pick = mirror_pick(HALF, side, side, 0)
    col_pick = mirror_pick(side, side, side, 0)
    live = lax.broadcasted_iota(jnp.int32, (HALF, side), 0) <= side // 2
    for n in range(ref.shape[0]):
        for part, sign in ((0, 1.0), (1, -1.0)):
            x = ref[n, part]
            both = 0.5 * (x[:HALF] + sign * mirrored(x, row_pick, col_pick))
            out[n, part] = jnp.where(live, both, 0.0)


def reference_half(references):
    count, _, side, _ = references.shape
    step = math.gcd(count, 4)
    return pl.pallas_call(
        functools.partial(reference_half_kernel, side),
        grid=(count // step,),
        in_specs=[pl.BlockSpec((step, 2, side, side), lambda i: (i, 0, 0, 0))],
        out_specs=pl.BlockSpec((step, 2, HALF, side), lambda i: (i, 0, 0, 0)),
        out_shape=jax.ShapeDtypeStruct((count, 2, HALF, side), f32),
        compiler_params=pltpu.CompilerParams(vmem_limit_bytes=VMEM_BYTES),
        cost_estimate=pl.CostEstimate(
            flops=count * 2 * 8 * HALF * side * side, bytes_accessed=count * 4 * 200 * side * 2,
            transcendentals=0,
        ),
        name="reference_half",
    )(references)


def owner_kernel(
    side, info, images, refs, contrast, phase, right_hi, right_lo, left_hi, left_lo,
    sr_hi, sr_lo, score_left, start, scores, total,
):
    @pl.when(pl.program_id(0) == 0)
    def _():
        total[...] = start[...]

    base = pl.program_id(0) * GROUP
    lane = lax.broadcasted_iota(jnp.int32, (8, side), 1)
    tail_row = lax.broadcasted_iota(jnp.int32, (8, side), 0)
    rows = []
    for n in range(GROUP):
        local, bin_at, shift = info[0, base + n], info[1, base + n], info[2, base + n]
        turns, live = info[3, base + n], info[4, base + n].astype(f32)
        image = images[n]
        image = jnp.where(turns % 2 == 1, image.T, image)
        right_at = (turns >= 2).astype(jnp.int32)
        left_at = ((turns == 1) | (turns == 2)).astype(jnp.int32)
        halfway = dot3(split(image), (right_hi[right_at], right_lo[right_at]))
        halfway = jnp.concatenate([halfway[:, :side], halfway[:, side:]], axis=0)
        spec = dot3((left_hi[left_at], left_lo[left_at]), split(halfway))
        gain = contrast[bin_at] * live
        re, im = spec[:HALF] * gain, spec[HALF:] * gain
        ref_re, ref_im = refs[local, 0], refs[local, 1]
        product = jnp.concatenate([re * ref_re + im * ref_im, im * ref_re - re * ref_im], axis=0)
        part = dot3(split(product), (sr_hi[...], sr_lo[...]))
        rows.append(jnp.sum(part * score_left[...], axis=0, keepdims=True))
        cos, sin = phase[shift, 0], phase[shift, 1]
        con_re, con_im = re * cos - im * sin, im * cos + re * sin
        tail = jnp.where((tail_row == 1) & (lane == bin_at), live, con_re[side // 2 :])
        total[local, : side // 2] += con_re[: side // 2]
        total[local, side // 2 : HALF] += tail
        total[local, HALF:] += con_im
    found = jnp.concatenate(rows, axis=0)
    scores[...] = found + pltpu.roll(found, found.shape[1] // 2, 1)


def owner_terms(images, info, start, refs, tables):
    count, side, _ = images.shape
    contrast, phase, right, left, score_right, score_left = tables
    whole = lambda x: pl.BlockSpec(
        x.shape, lambda i, info: (0,) * x.ndim, pipeline_mode=pl.Buffered(1)
    )
    fixed = (refs, contrast, phase, *right, *left, *score_right, score_left, start)
    lanes = score_left.shape[1]
    return pl.pallas_call(
        functools.partial(owner_kernel, side),
        grid_spec=pltpu.PrefetchScalarGridSpec(
            num_scalar_prefetch=1,
            grid=(count // GROUP,),
            in_specs=[pl.BlockSpec((GROUP, side, side), lambda i, info: (i, 0, 0))]
            + [whole(x) for x in fixed],
            out_specs=[
                pl.BlockSpec((GROUP, lanes), lambda i, info: (i, 0)),
                pl.BlockSpec(start.shape, lambda i, info: (0, 0, 0)),
            ],
        ),
        out_shape=[
            jax.ShapeDtypeStruct((count, lanes), f32),
            jax.ShapeDtypeStruct(start.shape, f32),
        ],
        compiler_params=pltpu.CompilerParams(vmem_limit_bytes=VMEM_BYTES),
        cost_estimate=pl.CostEstimate(
            flops=count * 70_000_000, bytes_accessed=count * side * side * 4 + 14_000_000,
            transcendentals=0,
        ),
        name="owner_terms",
    )(info, images, *fixed)


def finish_kernel(side, bins, share, contrast, out):
    row_pick = mirror_pick(side // 2, HALF, side, side // 2)
    col_pick = mirror_pick(side, side, side, 0)
    tail_row = lax.broadcasted_iota(jnp.int32, (8, side), 0)
    middle = side // 2
    for n in range(share.shape[0]):
        counts = share[n, middle + 1 : middle + 2]
        weight = jnp.ones((HALF, side), f32)
        for d in range(bins):
            weight += counts[:, d : d + 1] * (contrast[d] * contrast[d])
        live = lax.broadcasted_iota(jnp.int32, (HALF, side), 0) <= middle
        for part, sign in ((0, 1.0), (1, -1.0)):
            fresh = jnp.where(live, share[n, part * HALF : (part + 1) * HALF], 0.0) / weight
            other = sign * mirrored(fresh, row_pick, col_pick)
            out[n, part, :middle] = fresh[:middle]
            out[n, part, middle : middle + 8] = jnp.where(tail_row == 0, fresh[middle:], other[:8])
            out[n, part, middle + 8 :] = other[8:]


def finish(share, contrast):
    count, _, side = share.shape
    return pl.pallas_call(
        functools.partial(finish_kernel, side, contrast.shape[0]),
        out_shape=jax.ShapeDtypeStruct((count, 2, side, side), f32),
        compiler_params=pltpu.CompilerParams(vmem_limit_bytes=VMEM_BYTES),
        cost_estimate=pl.CostEstimate(
            flops=count * 20_000_000, bytes_accessed=4_000_000, transcendentals=0
        ),
        name="finish",
    )(share, contrast)


def body(
    particles, references, class_of, rotation_bin, shift_best, defocus_bin, shift_list, defocus
):
    side = particles.shape[-1]
    part_rows = particles.shape[0]
    class_local = references.shape[0]
    shifts = shift_list.shape[0]
    owners = lax.axis_size("cls")
    capacity = max(2, 2 * part_rows // owners)
    chunk = capacity // 2
    slot_total = owners * capacity

    owner_of = class_of // class_local
    before = jnp.arange(part_rows)[:, None] > jnp.arange(part_rows)[None, :]
    rank = jnp.sum((before & (owner_of[:, None] == owner_of[None, :])).astype(jnp.int32), axis=1)
    target = (rank // chunk) * (owners * chunk) + owner_of * chunk + rank % chunk
    hit = target[None, :] == jnp.arange(slot_total, dtype=jnp.int32)[:, None]
    values = jnp.stack(
        [class_of % class_local, defocus_bin, shift_best, rotation_bin, jnp.ones_like(class_of)]
    )
    info = jnp.sum(jnp.where(hit[None], values[:, None, :], 0), axis=2).astype(f32)
    source = jnp.sum(
        jnp.where(hit, jnp.arange(part_rows, dtype=jnp.int32)[None, :], 0), axis=1
    ).reshape(2, owners * chunk)
    send = [particles[source[h]].reshape(owners, chunk, side, side) for h in (0, 1)]

    exchange = lambda x: lax.all_to_all(x, "cls", split_axis=0, concat_axis=0, tiled=True)
    info = info.reshape(5, 2, owners, chunk).transpose(2, 1, 0, 3)
    got = [exchange(send[0])]
    info = exchange(info).astype(jnp.int32).transpose(1, 2, 0, 3).reshape(2, 5, owners * chunk)
    got.append(exchange(send[1]))

    right, left = dft_tables(side)
    contrast = contrast_half(defocus, side)
    phase, score_right, score_left = shift_tables(shift_list, side)
    tables = (contrast, phase, split_table(right), split_table(left), split_table(score_right), score_left)
    refs = reference_half(references)

    total = jnp.zeros((class_local, 2 * HALF, side), f32)
    found = []
    for h in (0, 1):
        scores, total = owner_terms(
            got[h].reshape(owners * chunk, side, side), info[h], total, refs, tables
        )
        found.append(scores[:, :shifts].reshape(owners, chunk, shifts))
    share = lax.psum_scatter(total, "grp", scatter_dimension=0, tiled=True)
    home = exchange(jnp.concatenate(found, axis=1))
    home = home.reshape(owners, 2, chunk, shifts).transpose(1, 0, 2, 3)
    scores = home.reshape(slot_total, shifts)[target]
    return scores, finish(share, contrast)


def solution(mesh):
    return jax.shard_map(
        body,
        mesh=mesh,
        in_specs=(
            P(("grp", "cls"), None, None),
            P("cls", None, None, None),
            P(("grp", "cls")),
            P(("grp", "cls")),
            P(("grp", "cls")),
            P(("grp", "cls")),
            P(),
            P(),
        ),
        out_specs=(P(("grp", "cls"), None), P(("cls", "grp"), None, None, None)),
        check_vma=False,
    )
```

```python
import functools
import math

import jax
import jax.numpy as jnp
from jax import lax
from jax.experimental import pallas as pl
from jax.experimental.pallas import tpu as pltpu
from jax.sharding import PartitionSpec as P

f32, bf16 = jnp.float32, jnp.bfloat16
HALF = 72
GROUP = 8
VMEM_BYTES = 56 * 1024 * 1024


def split(x):
    high = x.astype(bf16)
    return high, (x - high.astype(f32)).astype(bf16)


def split_table(x):
    high = lax.reduce_precision(x, 8, 7)
    return high.astype(bf16), lax.reduce_precision(x - high, 8, 7).astype(bf16)


def dot(a, b):
    return jnp.dot(a, b, preferred_element_type=f32)


def dot3(a, b):
    return dot(a[0], b[0]) + (dot(a[1], b[0]) + dot(a[0], b[1]))


def circle(turns, side):
    angles = (turns % side).astype(f32) * (2.0 * math.pi / side)
    return jnp.cos(angles), jnp.sin(angles)


def dft_tables(side):
    pixel = jnp.arange(side, dtype=jnp.int32)
    norm = 1.0 / math.sqrt(side)
    cos_table, sin_table = circle(pixel[:, None] * pixel[None, :], side)
    cos_table, sin_table = cos_table * norm, sin_table * norm
    flip_cos, flip_sin = circle(pixel[:, None] * (side - 1 - pixel)[None, :], side)
    flip_cos, flip_sin = flip_cos * norm, flip_sin * norm
    right = jnp.stack(
        [
            jnp.concatenate([cos_table, sin_table], axis=1),
            jnp.concatenate([flip_cos.T, flip_sin.T], axis=1),
        ]
    )
    live = (jnp.arange(HALF) <= side // 2)[:, None].astype(f32)

    def left(c, s):
        c, s = c[:HALF] * live, s[:HALF] * live
        return jnp.concatenate(
            [jnp.concatenate([c, -s], axis=1), jnp.concatenate([-s, -c], axis=1)], axis=0
        )

    return right, jnp.stack([left(cos_table, sin_table), left(flip_cos, flip_sin)])


def contrast_half(defocus, side):
    pixel = jnp.arange(side, dtype=jnp.int32)
    signed = jnp.where(pixel < side // 2, pixel, pixel - side).astype(f32)
    rows = signed[:HALF]
    radius = (rows[:, None] * rows[:, None] + signed[None, :] * signed[None, :]) / float(
        (side // 2) ** 2
    )
    phases = defocus[:, None, None] * radius[None]
    return -(0.995 * jnp.sin(phases) + 0.1 * jnp.cos(phases))


def shift_tables(shift_list, side):
    row_cos, row_sin = circle(
        shift_list[:, 0][:, None] * jnp.arange(HALF, dtype=jnp.int32)[None, :], side
    )
    col_cos, col_sin = circle(
        shift_list[:, 1][:, None] * jnp.arange(side, dtype=jnp.int32)[None, :], side
    )
    rc, rs = row_cos[:, :, None], row_sin[:, :, None]
    cc, cs = col_cos[:, None, :], col_sin[:, None, :]
    phase = jnp.stack([rc * cc - rs * cs, rs * cc + rc * cs], axis=1)
    score_right = jnp.concatenate([col_cos.T, col_sin.T], axis=1)
    row = jnp.arange(HALF)
    times = jnp.where(
        (row == 0) | (row == side // 2), 1.0, jnp.where(row < side // 2, 2.0, 0.0)
    ).astype(f32)[:, None] / side
    uc, us = row_cos.T * times, row_sin.T * times
    score_left = jnp.concatenate(
        [jnp.concatenate([uc, -us], axis=1), jnp.concatenate([-us, -uc], axis=1)], axis=0
    )
    return phase, score_right, score_left


def mirror_pick(rows, cols, side, offset):
    i = lax.broadcasted_iota(jnp.int32, (rows, cols), 0)
    j = lax.broadcasted_iota(jnp.int32, (rows, cols), 1)
    return jnp.where((i + j) % side == offset, 1.0, 0.0).astype(bf16)


def mirrored(x, row_pick, col_pick):
    total = None
    for piece in split(x):
        turned = dot(dot(row_pick, piece).astype(bf16), col_pick)
        total = turned if total is None else total + turned
    return total


def reference_half_kernel(side, ref, out):
    row_pick = mirror_pick(HALF, side, side, 0)
    col_pick = mirror_pick(side, side, side, 0)
    live = lax.broadcasted_iota(jnp.int32, (HALF, side), 0) <= side // 2
    for n in range(ref.shape[0]):
        for part, sign in ((0, 1.0), (1, -1.0)):
            x = ref[n, part]
            both = 0.5 * (x[:HALF] + sign * mirrored(x, row_pick, col_pick))
            out[n, part] = jnp.where(live, both, 0.0)


def reference_half(references):
    count, _, side, _ = references.shape
    step = math.gcd(count, 4)
    return pl.pallas_call(
        functools.partial(reference_half_kernel, side),
        grid=(count // step,),
        in_specs=[pl.BlockSpec((step, 2, side, side), lambda i: (i, 0, 0, 0))],
        out_specs=pl.BlockSpec((step, 2, HALF, side), lambda i: (i, 0, 0, 0)),
        out_shape=jax.ShapeDtypeStruct((count, 2, HALF, side), f32),
        compiler_params=pltpu.CompilerParams(vmem_limit_bytes=VMEM_BYTES),
        cost_estimate=pl.CostEstimate(
            flops=count * 2 * 8 * HALF * side * side, bytes_accessed=count * 4 * 200 * side * 2,
            transcendentals=0,
        ),
        name="reference_half",
    )(references)


def owner_kernel(
    side, info, images, refs, contrast, phase, right_hi, right_lo, left_hi, left_lo,
    sr_hi, sr_lo, score_left, start, scores, total,
):
    @pl.when(pl.program_id(0) == 0)
    def _():
        total[...] = start[...]

    base = pl.program_id(0) * GROUP
    lane = lax.broadcasted_iota(jnp.int32, (8, side), 1)
    tail_row = lax.broadcasted_iota(jnp.int32, (8, side), 0)
    rows = []
    for n in range(GROUP):
        local, bin_at, shift = info[0, base + n], info[1, base + n], info[2, base + n]
        turns, live = info[3, base + n], info[4, base + n].astype(f32)
        image = images[n]
        image = jnp.where(turns % 2 == 1, image.T, image)
        right_at = (turns >= 2).astype(jnp.int32)
        left_at = ((turns == 1) | (turns == 2)).astype(jnp.int32)
        halfway = dot3(split(image), (right_hi[right_at], right_lo[right_at]))
        halfway = jnp.concatenate([halfway[:, :side], halfway[:, side:]], axis=0)
        spec = dot3((left_hi[left_at], left_lo[left_at]), split(halfway))
        gain = contrast[bin_at] * live
        re, im = spec[:HALF] * gain, spec[HALF:] * gain
        ref_re, ref_im = refs[local, 0], refs[local, 1]
        product = jnp.concatenate([re * ref_re + im * ref_im, im * ref_re - re * ref_im], axis=0)
        part = dot3(split(product), (sr_hi[...], sr_lo[...]))
        rows.append(jnp.sum(part * score_left[...], axis=0, keepdims=True))
        cos, sin = phase[shift, 0], phase[shift, 1]
        con_re, con_im = re * cos - im * sin, im * cos + re * sin
        tail = jnp.where((tail_row == 1) & (lane == bin_at), live, con_re[side // 2 :])
        total[local, : side // 2] += con_re[: side // 2]
        total[local, side // 2 : HALF] += tail
        total[local, HALF:] += con_im
    found = jnp.concatenate(rows, axis=0)
    scores[...] = found + pltpu.roll(found, found.shape[1] // 2, 1)


def owner_terms(images, info, start, refs, tables):
    count, side, _ = images.shape
    contrast, phase, right, left, score_right, score_left = tables
    whole = lambda x: pl.BlockSpec(
        x.shape, lambda i, info: (0,) * x.ndim, pipeline_mode=pl.Buffered(1)
    )
    fixed = (refs, contrast, phase, *right, *left, *score_right, score_left, start)
    lanes = score_left.shape[1]
    return pl.pallas_call(
        functools.partial(owner_kernel, side),
        grid_spec=pltpu.PrefetchScalarGridSpec(
            num_scalar_prefetch=1,
            grid=(count // GROUP,),
            in_specs=[pl.BlockSpec((GROUP, side, side), lambda i, info: (i, 0, 0))]
            + [whole(x) for x in fixed],
            out_specs=[
                pl.BlockSpec((GROUP, lanes), lambda i, info: (i, 0)),
                pl.BlockSpec(start.shape, lambda i, info: (0, 0, 0)),
            ],
        ),
        out_shape=[
            jax.ShapeDtypeStruct((count, lanes), f32),
            jax.ShapeDtypeStruct(start.shape, f32),
        ],
        compiler_params=pltpu.CompilerParams(vmem_limit_bytes=VMEM_BYTES),
        cost_estimate=pl.CostEstimate(
            flops=count * 70_000_000, bytes_accessed=count * side * side * 4 + 14_000_000,
            transcendentals=0,
        ),
        name="owner_terms",
    )(info, images, *fixed)


def finish_kernel(side, bins, share, contrast, out):
    row_pick = mirror_pick(side // 2, HALF, side, side // 2)
    col_pick = mirror_pick(side, side, side, 0)
    tail_row = lax.broadcasted_iota(jnp.int32, (8, side), 0)
    middle = side // 2
    for n in range(share.shape[0]):
        counts = share[n, middle + 1 : middle + 2]
        weight = jnp.ones((HALF, side), f32)
        for d in range(bins):
            weight += counts[:, d : d + 1] * (contrast[d] * contrast[d])
        live = lax.broadcasted_iota(jnp.int32, (HALF, side), 0) <= middle
        for part, sign in ((0, 1.0), (1, -1.0)):
            fresh = jnp.where(live, share[n, part * HALF : (part + 1) * HALF], 0.0) / weight
            other = sign * mirrored(fresh, row_pick, col_pick)
            out[n, part, :middle] = fresh[:middle]
            out[n, part, middle : middle + 8] = jnp.where(tail_row == 0, fresh[middle:], other[:8])
            out[n, part, middle + 8 :] = other[8:]


def finish(share, contrast):
    count, _, side = share.shape
    return pl.pallas_call(
        functools.partial(finish_kernel, side, contrast.shape[0]),
        out_shape=jax.ShapeDtypeStruct((count, 2, side, side), f32),
        compiler_params=pltpu.CompilerParams(vmem_limit_bytes=VMEM_BYTES),
        cost_estimate=pl.CostEstimate(
            flops=count * 20_000_000, bytes_accessed=4_000_000, transcendentals=0
        ),
        name="finish",
    )(share, contrast)


def body(
    particles, references, class_of, rotation_bin, shift_best, defocus_bin, shift_list, defocus
):
    side = particles.shape[-1]
    part_rows = particles.shape[0]
    class_local = references.shape[0]
    shifts = shift_list.shape[0]
    owners = lax.axis_size("cls")
    capacity = max(2, 2 * part_rows // owners)
    last = max(1, capacity // 4)
    chunks = (capacity - last, last)
    starts = (0, owners * chunks[0])
    slot_total = owners * capacity

    def places(classes):
        owner = classes // class_local
        rows = jnp.arange(part_rows)
        before = rows[:, None] > rows[None, :]
        same = owner[..., :, None] == owner[..., None, :]
        return owner, jnp.sum((before & same).astype(jnp.int32), axis=-1)

    owner_of, rank = places(class_of)
    target = jnp.where(
        rank < chunks[0],
        owner_of * chunks[0] + rank,
        starts[1] + owner_of * chunks[1] + rank - chunks[0],
    )
    hit = target[None, :] == jnp.arange(slot_total, dtype=jnp.int32)[:, None]
    source = jnp.sum(jnp.where(hit, jnp.arange(part_rows, dtype=jnp.int32)[None, :], 0), axis=1)
    send = [
        particles[source[s : s + owners * c]].reshape(owners, c, side, side)
        for s, c in zip(starts, chunks)
    ]

    exchange = lambda x: lax.all_to_all(x, "cls", split_axis=0, concat_axis=0, tiled=True)
    right, left = dft_tables(side)
    contrast = contrast_half(defocus, side)
    phase, score_right, score_left = shift_tables(shift_list, side)
    tables = (contrast, phase, split_table(right), split_table(left), split_table(score_right), score_left)
    refs = reference_half(references)
    got = [exchange(send[0])]
    got[0], send[1], refs, tables = lax.optimization_barrier((got[0], send[1], refs, tables))
    got.append(exchange(send[1]))

    facts = jnp.stack([class_of, defocus_bin, shift_best, rotation_bin]).astype(f32)
    facts = lax.all_gather(facts, "cls", axis=0).astype(jnp.int32).transpose(1, 0, 2)
    from_owner, from_rank = places(facts[0])
    mine = from_owner == lax.axis_index("cls")
    values = jnp.stack([facts[0] % class_local, facts[1], facts[2], facts[3], jnp.ones_like(facts[0])])

    def slot_info(first, count):
        slot = first + jnp.arange(count, dtype=jnp.int32)
        found = mine[:, None, :] & (from_rank[:, None, :] == slot[None, :, None])
        return jnp.sum(jnp.where(found[None], values[:, :, None, :], 0), axis=-1).reshape(5, -1)

    info = [slot_info(0, chunks[0]), slot_info(chunks[0], chunks[1])]

    total = jnp.zeros((class_local, 2 * HALF, side), f32)
    found = []
    for h in (0, 1):
        scores, total = owner_terms(got[h].reshape(-1, side, side), info[h], total, refs, tables)
        found.append(scores[:, :shifts].reshape(owners, chunks[h], shifts))
    share = lax.psum_scatter(total, "grp", scatter_dimension=0, tiled=True)
    home = exchange(jnp.concatenate(found, axis=1)).reshape(slot_total, shifts)
    scores = home[owner_of * capacity + rank]
    return scores, finish(share, contrast)


def solution(mesh):
    return jax.shard_map(
        body,
        mesh=mesh,
        in_specs=(
            P(("grp", "cls"), None, None),
            P("cls", None, None, None),
            P(("grp", "cls")),
            P(("grp", "cls")),
            P(("grp", "cls")),
            P(("grp", "cls")),
            P(),
            P(),
        ),
        out_specs=(P(("grp", "cls"), None), P(("cls", "grp"), None, None, None)),
        check_vma=False,
    )
```

```python
import functools
import math

import jax
import jax.numpy as jnp
from jax import lax
from jax.experimental import pallas as pl
from jax.experimental.pallas import tpu as pltpu
from jax.sharding import PartitionSpec as P

f32, bf16 = jnp.float32, jnp.bfloat16
HALF = 72
GROUP = 8
VMEM_BYTES = 56 * 1024 * 1024


def split(x):
    high = x.astype(bf16)
    return high, (x - high.astype(f32)).astype(bf16)


def split_table(x):
    high = lax.reduce_precision(x, 8, 7)
    return high.astype(bf16), lax.reduce_precision(x - high, 8, 7).astype(bf16)


def dot(a, b):
    return jnp.dot(a, b, preferred_element_type=f32)


def dot3(a, b):
    return dot(a[0], b[0]) + (dot(a[1], b[0]) + dot(a[0], b[1]))


def circle(turns, side):
    angles = (turns % side).astype(f32) * (2.0 * math.pi / side)
    return jnp.cos(angles), jnp.sin(angles)


def dft_tables(side):
    pixel = jnp.arange(side, dtype=jnp.int32)
    norm = 1.0 / math.sqrt(side)
    cos_table, sin_table = circle(pixel[:, None] * pixel[None, :], side)
    cos_table, sin_table = cos_table * norm, sin_table * norm
    flip_cos, flip_sin = circle(pixel[:, None] * (side - 1 - pixel)[None, :], side)
    flip_cos, flip_sin = flip_cos * norm, flip_sin * norm
    right = jnp.stack(
        [
            jnp.concatenate([cos_table, sin_table], axis=1),
            jnp.concatenate([flip_cos.T, flip_sin.T], axis=1),
        ]
    )
    live = (jnp.arange(HALF) <= side // 2)[:, None].astype(f32)

    def left(c, s):
        c, s = c[:HALF] * live, s[:HALF] * live
        return jnp.concatenate(
            [jnp.concatenate([c, -s], axis=1), jnp.concatenate([-s, -c], axis=1)], axis=0
        )

    return right, jnp.stack([left(cos_table, sin_table), left(flip_cos, flip_sin)])


def contrast_half(defocus, side):
    pixel = jnp.arange(side, dtype=jnp.int32)
    signed = jnp.where(pixel < side // 2, pixel, pixel - side).astype(f32)
    rows = signed[:HALF]
    radius = (rows[:, None] * rows[:, None] + signed[None, :] * signed[None, :]) / float(
        (side // 2) ** 2
    )
    phases = defocus[:, None, None] * radius[None]
    return -(0.995 * jnp.sin(phases) + 0.1 * jnp.cos(phases))


def shift_tables(shift_list, side):
    row_cos, row_sin = circle(
        shift_list[:, 0][:, None] * jnp.arange(HALF, dtype=jnp.int32)[None, :], side
    )
    col_cos, col_sin = circle(
        shift_list[:, 1][:, None] * jnp.arange(side, dtype=jnp.int32)[None, :], side
    )
    rc, rs = row_cos[:, :, None], row_sin[:, :, None]
    cc, cs = col_cos[:, None, :], col_sin[:, None, :]
    phase = jnp.stack([rc * cc - rs * cs, rs * cc + rc * cs], axis=1)
    score_right = jnp.concatenate([col_cos.T, col_sin.T], axis=1)
    row = jnp.arange(HALF)
    times = jnp.where(
        (row == 0) | (row == side // 2), 1.0, jnp.where(row < side // 2, 2.0, 0.0)
    ).astype(f32)[:, None] / side
    uc, us = row_cos.T * times, row_sin.T * times
    score_left = jnp.concatenate(
        [jnp.concatenate([uc, -us], axis=1), jnp.concatenate([-us, -uc], axis=1)], axis=0
    )
    return phase, score_right, score_left


def mirror_pick(rows, cols, side, offset):
    i = lax.broadcasted_iota(jnp.int32, (rows, cols), 0)
    j = lax.broadcasted_iota(jnp.int32, (rows, cols), 1)
    return jnp.where((i + j) % side == offset, 1.0, 0.0).astype(bf16)


def mirrored(x, row_pick, col_pick):
    total = None
    for piece in split(x):
        turned = dot(dot(row_pick, piece).astype(bf16), col_pick)
        total = turned if total is None else total + turned
    return total


def reference_half_kernel(side, ref, out):
    row_pick = mirror_pick(HALF, side, side, 0)
    col_pick = mirror_pick(side, side, side, 0)
    live = lax.broadcasted_iota(jnp.int32, (HALF, side), 0) <= side // 2
    for n in range(ref.shape[0]):
        for part, sign in ((0, 1.0), (1, -1.0)):
            x = ref[n, part]
            both = 0.5 * (x[:HALF] + sign * mirrored(x, row_pick, col_pick))
            out[n, part] = jnp.where(live, both, 0.0)


def reference_half(references):
    count, _, side, _ = references.shape
    step = math.gcd(count, 4)
    return pl.pallas_call(
        functools.partial(reference_half_kernel, side),
        grid=(count // step,),
        in_specs=[pl.BlockSpec((step, 2, side, side), lambda i: (i, 0, 0, 0))],
        out_specs=pl.BlockSpec((step, 2, HALF, side), lambda i: (i, 0, 0, 0)),
        out_shape=jax.ShapeDtypeStruct((count, 2, HALF, side), f32),
        compiler_params=pltpu.CompilerParams(vmem_limit_bytes=VMEM_BYTES),
        cost_estimate=pl.CostEstimate(
            flops=count * 2 * 8 * HALF * side * side, bytes_accessed=count * 4 * 200 * side * 2,
            transcendentals=0,
        ),
        name="reference_half",
    )(references)


def owner_kernel(
    side, info, images, refs, contrast, phase, right_hi, right_lo, left_hi, left_lo,
    sr_hi, sr_lo, score_left, start, scores, total,
):
    @pl.when(pl.program_id(0) == 0)
    def _():
        total[...] = start[...]

    group = scores.shape[1]
    per_source = group // images.shape[0]
    base = pl.program_id(0) * group
    lane = lax.broadcasted_iota(jnp.int32, (8, side), 1)
    tail_row = lax.broadcasted_iota(jnp.int32, (8, side), 0)
    rows = []
    for n in range(group):
        local, bin_at, shift = info[0, base + n], info[1, base + n], info[2, base + n]
        turns, live = info[3, base + n], info[4, base + n].astype(f32)
        at = n % per_source * side
        image = images[n // per_source, at : at + side]
        image = jnp.where(turns % 2 == 1, image.T, image)
        right_at = (turns >= 2).astype(jnp.int32)
        left_at = ((turns == 1) | (turns == 2)).astype(jnp.int32)
        halfway = dot3(split(image), (right_hi[right_at], right_lo[right_at]))
        halfway = jnp.concatenate([halfway[:, :side], halfway[:, side:]], axis=0)
        spec = dot3((left_hi[left_at], left_lo[left_at]), split(halfway))
        gain = contrast[bin_at] * live
        re, im = spec[:HALF] * gain, spec[HALF:] * gain
        ref_re, ref_im = refs[local, 0], refs[local, 1]
        product = jnp.concatenate([re * ref_re + im * ref_im, im * ref_re - re * ref_im], axis=0)
        part = dot3(split(product), (sr_hi[...], sr_lo[...]))
        rows.append(jnp.sum(part * score_left[...], axis=0, keepdims=True))
        cos, sin = phase[shift, 0], phase[shift, 1]
        con_re, con_im = re * cos - im * sin, im * cos + re * sin
        tail = jnp.where((tail_row == 1) & (lane == bin_at), live, con_re[side // 2 :])
        total[local, : side // 2] += con_re[: side // 2]
        total[local, side // 2 : HALF] += tail
        total[local, HALF:] += con_im
    found = jnp.concatenate(rows, axis=0)
    scores[0] = found + pltpu.roll(found, found.shape[1] // 2, 1)


def owner_terms(images, info, start, refs, tables):
    sources, held, side = images.shape
    per_source = held // side
    count = sources * per_source
    block = math.gcd(sources, max(1, GROUP // per_source))
    group = block * per_source
    contrast, phase, right, left, score_right, score_left = tables
    whole = lambda x: pl.BlockSpec(
        x.shape, lambda i, info: (0,) * x.ndim, pipeline_mode=pl.Buffered(1)
    )
    fixed = (refs, contrast, phase, *right, *left, *score_right, score_left, start)
    lanes = score_left.shape[1]
    return pl.pallas_call(
        functools.partial(owner_kernel, side),
        grid_spec=pltpu.PrefetchScalarGridSpec(
            num_scalar_prefetch=1,
            grid=(sources // block,),
            in_specs=[pl.BlockSpec((block, held, side), lambda i, info: (i, 0, 0))]
            + [whole(x) for x in fixed],
            out_specs=[
                pl.BlockSpec((1, group, lanes), lambda i, info: (i, 0, 0)),
                pl.BlockSpec(start.shape, lambda i, info: (0, 0, 0)),
            ],
        ),
        out_shape=[
            jax.ShapeDtypeStruct((sources // block, group, lanes), f32),
            jax.ShapeDtypeStruct(start.shape, f32),
        ],
        compiler_params=pltpu.CompilerParams(vmem_limit_bytes=VMEM_BYTES),
        cost_estimate=pl.CostEstimate(
            flops=count * 70_000_000, bytes_accessed=count * side * side * 4 + 14_000_000,
            transcendentals=0,
        ),
        name="owner_terms",
    )(info, images, *fixed)


def finish_class(side, bins, share, contrast, out, n):
    row_pick = mirror_pick(side // 2, HALF, side, side // 2)
    col_pick = mirror_pick(side, side, side, 0)
    tail_row = lax.broadcasted_iota(jnp.int32, (8, side), 0)
    middle = side // 2
    counts = share[middle + 1 : middle + 2]
    weight = jnp.ones((HALF, side), f32)
    for d in range(bins):
        weight += counts[:, d : d + 1] * (contrast[d] * contrast[d])
    live = lax.broadcasted_iota(jnp.int32, (HALF, side), 0) <= middle
    for part, sign in ((0, 1.0), (1, -1.0)):
        fresh = jnp.where(live, share[part * HALF : (part + 1) * HALF], 0.0) / weight
        other = sign * mirrored(fresh, row_pick, col_pick)
        out[n, part, :middle] = fresh[:middle]
        out[n, part, middle : middle + 8] = jnp.where(tail_row == 0, fresh[middle:], other[:8])
        out[n, part, middle + 8 :] = other[8:]


def close_kernel(
    side, bins, groups, owners, total, found, contrast, out, home,
    near, mid, far, board, near_send, near_recv, far_send, far_recv, score_send, score_recv,
):
    mesh_ids = pl.DeviceIdType.MESH
    grp, cls = lax.axis_index("grp"), lax.axis_index("cls")
    row, core = grp // 2, grp % 2
    rows = groups // 2
    pieces = near_send.shape[1]
    per = total.shape[2]
    size = per // pieces
    partner = 2 * row + (1 - core)
    row_at = [lax.rem(row + d, rows) for d in range(rows)]
    cls_at = [lax.rem(cls + d, owners) for d in range(owners)]

    barrier = pltpu.get_barrier_semaphore()
    greet = [{"grp": partner}] + [{"grp": 2 * row_at[d] + core} for d in range(1, rows)]
    greet += [{"cls": cls_at[d]} for d in range(1, owners)]
    for device in greet:
        pl.semaphore_signal(barrier, inc=1, device_id=device, device_id_type=mesh_ids)
    pl.semaphore_wait(barrier, len(greet))

    def copy(source, target, send, recv, device):
        made = pltpu.make_async_remote_copy(
            src_ref=source, dst_ref=target, send_sem=send, recv_sem=recv,
            device_id=device, device_id_type=mesh_ids,
        )
        made.start()
        return made

    order = [(d, q) for d in list(range(1, rows)) + [0] for q in range(pieces)]
    near_copies, far_copies = {}, {}
    for d, q in order:
        span = pl.ds(q * size, size)
        near_copies[d, q] = copy(
            total.at[row_at[d], 1 - core, span], near.at[d, span],
            near_send.at[d, q], near_recv.at[d, q], {"grp": partner},
        )
    for d, q in order:
        near_copies[d, q].wait()
        if d == 0:
            continue
        span = pl.ds(q * size, size)
        mid[d - 1, span] = total[row_at[d], core, span] + near[d, span]
        far_copies[d, q] = copy(
            mid.at[d - 1, span], far.at[d - 1, span],
            far_send.at[d - 1, q], far_recv.at[d - 1, q], {"grp": 2 * row_at[d] + core},
        )
    score_copies = [
        copy(
            found.at[cls_at[d]], board.at[cls],
            score_send.at[d], score_recv.at[d], {"cls": cls_at[d]},
        )
        for d in range(1, owners)
    ]
    for q in range(pieces):
        for d in range(1, rows):
            far_copies[d, q].wait()
        for n in range(q * size, (q + 1) * size):
            share = total[row, core, n] + near[0, n]
            for d in range(1, rows):
                share = share + far[d - 1, n]
            finish_class(side, bins, share, contrast, out, n)
    for made in score_copies:
        made.wait()
    board[cls] = found[cls]
    home[...] = board[...]


def close(total, found, contrast, groups, owners):
    class_local, height, side = total.shape
    rows, per = groups // 2, class_local // groups
    pieces = math.gcd(per, 2)
    dma = pltpu.SemaphoreType.DMA
    vmem = pl.BlockSpec(memory_space=pltpu.VMEM)
    return pl.pallas_call(
        functools.partial(close_kernel, side, contrast.shape[0], groups, owners),
        in_specs=[vmem] * 3,
        out_specs=[vmem] * 2,
        out_shape=[
            jax.ShapeDtypeStruct((per, 2, side, side), f32),
            jax.ShapeDtypeStruct(found.shape, f32),
        ],
        scratch_shapes=[
            pltpu.VMEM((rows, per, height, side), f32),
            pltpu.VMEM((max(1, rows - 1), per, height, side), f32),
            pltpu.VMEM((max(1, rows - 1), per, height, side), f32),
            pltpu.VMEM(found.shape, f32),
            dma((rows, pieces)),
            dma((rows, pieces)),
            dma((max(1, rows - 1), pieces)),
            dma((max(1, rows - 1), pieces)),
            dma((owners,)),
            dma((owners,)),
        ],
        compiler_params=pltpu.CompilerParams(
            collective_id=0, has_side_effects=True, vmem_limit_bytes=VMEM_BYTES
        ),
        cost_estimate=pl.CostEstimate(
            flops=per * 20_000_000, bytes_accessed=8_000_000, transcendentals=0
        ),
        name="close",
    )(total.reshape(rows, 2, per, height, side), found, contrast)


def body(
    particles, references, class_of, rotation_bin, shift_best, defocus_bin, shift_list, defocus
):
    side = particles.shape[-1]
    part_rows = particles.shape[0]
    class_local = references.shape[0]
    shifts = shift_list.shape[0]
    owners = lax.axis_size("cls")
    capacity = max(2, 2 * part_rows // owners)
    last = max(1, capacity // 4)
    chunks = (capacity - last, last)
    starts = (0, owners * chunks[0])
    slot_total = owners * capacity

    def places(classes):
        owner = classes // class_local
        rows = jnp.arange(part_rows)
        before = rows[:, None] > rows[None, :]
        same = owner[..., :, None] == owner[..., None, :]
        return owner, jnp.sum((before & same).astype(jnp.int32), axis=-1)

    owner_of, rank = places(class_of)
    target = jnp.where(
        rank < chunks[0],
        owner_of * chunks[0] + rank,
        starts[1] + owner_of * chunks[1] + rank - chunks[0],
    )
    hit = target[None, :] == jnp.arange(slot_total, dtype=jnp.int32)[:, None]
    source = jnp.sum(jnp.where(hit, jnp.arange(part_rows, dtype=jnp.int32)[None, :], 0), axis=1)
    send = [
        particles[source[s : s + owners * c]].reshape(owners, c * side, side)
        for s, c in zip(starts, chunks)
    ]
    facts = jnp.stack(
        [class_of % class_local, defocus_bin, shift_best, rotation_bin, jnp.ones_like(class_of)]
    )
    place = (owner_of * capacity + rank)[None, :] == jnp.arange(slot_total, dtype=jnp.int32)[:, None]
    facts = jnp.sum(jnp.where(place[None], facts[:, None, :], 0), axis=2).astype(f32)
    facts = facts.reshape(5, owners, capacity).transpose(1, 0, 2)
    facts = jnp.pad(facts, ((0, 0), (0, 3), (0, side - capacity)))
    send[0] = jnp.concatenate([send[0], facts], axis=1)

    exchange = lambda x: lax.all_to_all(x, "cls", split_axis=0, concat_axis=0, tiled=True)
    right, left = dft_tables(side)
    contrast = contrast_half(defocus, side)
    phase, score_right, score_left = shift_tables(shift_list, side)
    tables = (contrast, phase, split_table(right), split_table(left), split_table(score_right), score_left)
    refs = reference_half(references)
    got = [exchange(send[0])]
    got[0], send[1], refs, tables = lax.optimization_barrier((got[0], send[1], refs, tables))
    got.append(exchange(send[1]))

    facts = got[0][:, chunks[0] * side : chunks[0] * side + 5, :capacity].astype(jnp.int32)
    facts = facts.transpose(1, 0, 2)
    info = [
        facts[:, :, : chunks[0]].reshape(5, -1),
        facts[:, :, chunks[0] :].reshape(5, -1),
    ]

    total = jnp.zeros((class_local, 2 * HALF, side), f32)
    found = []
    for h in (0, 1):
        scores, total = owner_terms(got[h], info[h], total, refs, tables)
        found.append(scores.reshape(owners, chunks[h], -1))
    found = jnp.concatenate(found, axis=1)
    fresh, home = close(total, found, contrast, lax.axis_size("grp"), owners)
    home = home.reshape(slot_total, -1)
    return home[owner_of * capacity + rank][:, :shifts], fresh


def solution(mesh):
    return jax.shard_map(
        body,
        mesh=mesh,
        in_specs=(
            P(("grp", "cls"), None, None),
            P("cls", None, None, None),
            P(("grp", "cls")),
            P(("grp", "cls")),
            P(("grp", "cls")),
            P(("grp", "cls")),
            P(),
            P(),
        ),
        out_specs=(P(("grp", "cls"), None), P(("cls", "grp"), None, None, None)),
        check_vma=False,
    )
```

```python
import functools
import math

import jax
import jax.numpy as jnp
from jax import lax
from jax.experimental import pallas as pl
from jax.experimental.pallas import tpu as pltpu
from jax.sharding import PartitionSpec as P

f32, bf16 = jnp.float32, jnp.bfloat16
HALF = 72
GROUP = 8
VMEM_BYTES = 56 * 1024 * 1024


def split(x):
    high = x.astype(bf16)
    return high, (x - high.astype(f32)).astype(bf16)


def split_table(x):
    high = lax.reduce_precision(x, 8, 7)
    return high.astype(bf16), lax.reduce_precision(x - high, 8, 7).astype(bf16)


def dot(a, b):
    return jnp.dot(a, b, preferred_element_type=f32)


def dot3(a, b):
    return dot(a[0], b[0]) + (dot(a[1], b[0]) + dot(a[0], b[1]))


def circle(turns, side):
    angles = (turns % side).astype(f32) * (2.0 * math.pi / side)
    return jnp.cos(angles), jnp.sin(angles)


def dft_tables(side):
    pixel = jnp.arange(side, dtype=jnp.int32)
    norm = 1.0 / math.sqrt(side)
    cos_table, sin_table = circle(pixel[:, None] * pixel[None, :], side)
    cos_table, sin_table = cos_table * norm, sin_table * norm
    flip_cos, flip_sin = circle(pixel[:, None] * (side - 1 - pixel)[None, :], side)
    flip_cos, flip_sin = flip_cos * norm, flip_sin * norm
    right = jnp.stack(
        [
            jnp.concatenate([cos_table, sin_table], axis=1),
            jnp.concatenate([flip_cos.T, flip_sin.T], axis=1),
        ]
    )
    live = (jnp.arange(HALF) <= side // 2)[:, None].astype(f32)

    def left(c, s):
        c, s = c[:HALF] * live, s[:HALF] * live
        return jnp.concatenate(
            [jnp.concatenate([c, -s], axis=1), jnp.concatenate([-s, -c], axis=1)], axis=0
        )

    return right, jnp.stack([left(cos_table, sin_table), left(flip_cos, flip_sin)])


def contrast_half(defocus, side):
    pixel = jnp.arange(side, dtype=jnp.int32)
    signed = jnp.where(pixel < side // 2, pixel, pixel - side).astype(f32)
    rows = signed[:HALF]
    radius = (rows[:, None] * rows[:, None] + signed[None, :] * signed[None, :]) / float(
        (side // 2) ** 2
    )
    phases = defocus[:, None, None] * radius[None]
    return -(0.995 * jnp.sin(phases) + 0.1 * jnp.cos(phases))


def shift_tables(shift_list, side):
    row_cos, row_sin = circle(
        shift_list[:, 0][:, None] * jnp.arange(HALF, dtype=jnp.int32)[None, :], side
    )
    col_cos, col_sin = circle(
        shift_list[:, 1][:, None] * jnp.arange(side, dtype=jnp.int32)[None, :], side
    )
    rc, rs = row_cos[:, :, None], row_sin[:, :, None]
    cc, cs = col_cos[:, None, :], col_sin[:, None, :]
    phase = jnp.stack([rc * cc - rs * cs, rs * cc + rc * cs], axis=1)
    score_right = jnp.concatenate([col_cos.T, col_sin.T], axis=1)
    row = jnp.arange(HALF)
    times = jnp.where(
        (row == 0) | (row == side // 2), 1.0, jnp.where(row < side // 2, 2.0, 0.0)
    ).astype(f32)[:, None] / side
    uc, us = row_cos.T * times, row_sin.T * times
    score_left = jnp.concatenate(
        [jnp.concatenate([uc, -us], axis=1), jnp.concatenate([-us, -uc], axis=1)], axis=0
    )
    return phase, score_right, score_left


def mirror_pick(rows, cols, side, offset):
    i = lax.broadcasted_iota(jnp.int32, (rows, cols), 0)
    j = lax.broadcasted_iota(jnp.int32, (rows, cols), 1)
    return jnp.where((i + j) % side == offset, 1.0, 0.0).astype(bf16)


def mirrored(x, row_pick, col_pick):
    total = None
    for piece in split(x):
        turned = dot(dot(row_pick, piece).astype(bf16), col_pick)
        total = turned if total is None else total + turned
    return total


def gather_kernel(
    side, owners, chunks, info, last, send, references, phase_in, contrast,
    right_hi, right_lo, left_hi, left_lo, sr_hi, sr_lo, score_left, scores, total,
    got, held_refs, phase, refs, running, send_sem, recv_sem, local_sem,
):
    mesh_ids = pl.DeviceIdType.MESH
    cls = lax.axis_index("cls")
    slots = scores.shape[2]
    span = slots * side
    classes = refs.shape[0]

    local_copies = [
        pltpu.make_async_copy(references, held_refs, local_sem.at[0]),
        pltpu.make_async_copy(phase_in, phase, local_sem.at[1]),
        pltpu.make_async_copy(send.at[cls], got.at[cls], local_sem.at[2]),
    ]

    def copy(r, d):
        to = lax.rem(cls + d, owners)
        rows = pl.ds(pl.multiple_of(r * span, side), span)
        return pltpu.make_async_remote_copy(
            src_ref=send.at[to, rows], dst_ref=got.at[cls, rows],
            send_sem=send_sem.at[r, d], recv_sem=recv_sem.at[r, d],
            device_id={"cls": to}, device_id_type=mesh_ids,
        )

    barrier = pltpu.get_barrier_semaphore()
    for d in range(1, owners):
        pl.semaphore_signal(
            barrier, inc=1, device_id={"cls": lax.rem(cls + d, owners)}, device_id_type=mesh_ids
        )
    for made in local_copies:
        made.start()
    pl.semaphore_wait(barrier, owners - 1)
    for r in range(min(2, chunks)):
        for d in range(1, owners):
            copy(r, d).start()

    running[0] = jnp.zeros(running.shape[1:], f32)
    for made in local_copies:
        made.wait()
    row_pick = mirror_pick(HALF, side, side, 0)
    col_pick = mirror_pick(side, side, side, 0)
    live_row = lax.broadcasted_iota(jnp.int32, (HALF, side), 0) <= side // 2
    at_once = math.gcd(classes, 4)

    def halve(step, carry):
        for n in range(at_once):
            for part, sign in ((0, 1.0), (1, -1.0)):
                x = held_refs[step * at_once + n, part]
                both = 0.5 * (x[:HALF] + sign * mirrored(x, row_pick, col_pick))
                refs[step * at_once + n, part] = jnp.where(live_row, both, 0.0)
        return carry

    lax.fori_loop(0, classes // at_once, halve, 0)

    lane = lax.broadcasted_iota(jnp.int32, (8, side), 1)
    tail_row = lax.broadcasted_iota(jnp.int32, (8, side), 0)
    block = math.gcd(owners, max(1, GROUP // slots))

    def particle(at, image):
        bin_at, shift = info[1, at], info[2, at]
        local, turns, live = info[0, at], info[3, at], info[4, at].astype(f32)
        image = jnp.where(turns % 2 == 1, image.T, image)
        right_at = (turns >= 2).astype(jnp.int32)
        left_at = ((turns == 1) | (turns == 2)).astype(jnp.int32)
        halfway = dot3(split(image), (right_hi[right_at], right_lo[right_at]))
        halfway = jnp.concatenate([halfway[:, :side], halfway[:, side:]], axis=0)
        spec = dot3((left_hi[left_at], left_lo[left_at]), split(halfway))
        gain = contrast[bin_at] * live
        re, im = spec[:HALF] * gain, spec[HALF:] * gain
        ref_re, ref_im = refs[local, 0], refs[local, 1]
        product = jnp.concatenate([re * ref_re + im * ref_im, im * ref_re - re * ref_im], axis=0)
        part = dot3(split(product), (sr_hi[...], sr_lo[...]))
        score = jnp.sum(part * score_left[...], axis=0, keepdims=True)
        cos, sin = phase[shift, 0], phase[shift, 1]
        con_re, con_im = re * cos - im * sin, im * cos + re * sin
        tail = jnp.where((tail_row == 1) & (lane == bin_at), live, con_re[side // 2 :])
        return score, jnp.concatenate([con_re[: side // 2], tail, con_im], axis=0)

    def chunk(r, carry):
        for d in range(1, owners):
            copy(r, d).wait()

        @pl.when(r + 2 < chunks)
        def _():
            for d in range(1, owners):
                copy(r + 2, d).start()

        def sources(step, inner):
            base = (r * owners + step * block) * slots
            found, parts = [], []
            for n in range(block * slots):
                start = pl.multiple_of(r * span + n % slots * side, side)
                score, part = particle(
                    base + n, got[step * block + n // slots, pl.ds(start, side)]
                )
                found.append(score)
                parts.append(part)
            for n in range(block * slots):
                running[base + n + 1] = running[info[5, base + n]] + parts[n]
            found = jnp.concatenate(found, axis=0)
            found = found + pltpu.roll(found, found.shape[1] // 2, 1)
            for n in range(block):
                scores[r, step * block + n] = found[n * slots : (n + 1) * slots]
            return inner

        return lax.fori_loop(0, owners // block, sources, carry)

    lax.fori_loop(0, chunks, chunk, 0)

    def close_class(c, carry):
        total[c] = running[last[c]]
        return carry

    lax.fori_loop(0, classes, close_class, 0)


def gather_terms(send, info, last, references, tables, chunks):
    owners, held, side = send.shape
    slots = held // side // chunks
    class_local = references.shape[0]
    contrast, phase, right, left, score_right, score_left = tables
    lanes = score_left.shape[1]
    vmem = pl.BlockSpec(memory_space=pltpu.VMEM)
    smem = pl.BlockSpec(memory_space=pltpu.SMEM)
    hbm = pl.BlockSpec(memory_space=pl.ANY)
    dma = pltpu.SemaphoreType.DMA
    return pl.pallas_call(
        functools.partial(gather_kernel, side, owners, chunks),
        in_specs=[smem, smem, hbm, hbm, hbm] + [vmem] * 8,
        out_specs=[vmem, vmem],
        out_shape=[
            jax.ShapeDtypeStruct((chunks, owners, slots, lanes), f32),
            jax.ShapeDtypeStruct((class_local, 2 * HALF, side), f32),
        ],
        scratch_shapes=[
            pltpu.VMEM(send.shape, f32),
            pltpu.VMEM(references.shape, f32),
            pltpu.VMEM(phase.shape, f32),
            pltpu.VMEM((class_local, 2, HALF, side), f32),
            pltpu.VMEM((owners * slots * chunks + 1, 2 * HALF, side), f32),
            dma((chunks, owners)),
            dma((chunks, owners)),
            dma((3,)),
        ],
        compiler_params=pltpu.CompilerParams(
            collective_id=1, has_side_effects=True, vmem_limit_bytes=VMEM_BYTES
        ),
        cost_estimate=pl.CostEstimate(
            flops=owners * slots * chunks * 70_000_000, bytes_accessed=30_000_000,
            transcendentals=0,
        ),
        name="gather_terms",
    )(info, last, send, references, phase, contrast, *right, *left, *score_right, score_left)


def finish_class(side, bins, share, contrast, out, n):
    row_pick = mirror_pick(side // 2, HALF, side, side // 2)
    col_pick = mirror_pick(side, side, side, 0)
    tail_row = lax.broadcasted_iota(jnp.int32, (8, side), 0)
    middle = side // 2
    counts = share[middle + 1 : middle + 2]
    weight = jnp.ones((HALF, side), f32)
    for d in range(bins):
        weight += counts[:, d : d + 1] * (contrast[d] * contrast[d])
    live = lax.broadcasted_iota(jnp.int32, (HALF, side), 0) <= middle
    for part, sign in ((0, 1.0), (1, -1.0)):
        fresh = jnp.where(live, share[part * HALF : (part + 1) * HALF], 0.0) / weight
        other = sign * mirrored(fresh, row_pick, col_pick)
        out[n, part, :middle] = fresh[:middle]
        out[n, part, middle : middle + 8] = jnp.where(tail_row == 0, fresh[middle:], other[:8])
        out[n, part, middle + 8 :] = other[8:]


def close_kernel(
    side, bins, groups, owners, total, found, contrast, out, home,
    near, mid, far, board, near_send, near_recv, far_send, far_recv, score_send, score_recv,
):
    mesh_ids = pl.DeviceIdType.MESH
    grp, cls = lax.axis_index("grp"), lax.axis_index("cls")
    row, core = grp // 2, grp % 2
    rows = groups // 2
    pieces = near_send.shape[1]
    per = total.shape[2]
    size = per // pieces
    partner = 2 * row + (1 - core)
    row_at = [lax.rem(row + d, rows) for d in range(rows)]
    cls_at = [lax.rem(cls + d, owners) for d in range(owners)]

    barrier = pltpu.get_barrier_semaphore()
    greet = [{"grp": partner}] + [{"grp": 2 * row_at[d] + core} for d in range(1, rows)]
    greet += [{"cls": cls_at[d]} for d in range(1, owners)]
    for device in greet:
        pl.semaphore_signal(barrier, inc=1, device_id=device, device_id_type=mesh_ids)
    pl.semaphore_wait(barrier, len(greet))

    def copy(source, target, send, recv, device):
        made = pltpu.make_async_remote_copy(
            src_ref=source, dst_ref=target, send_sem=send, recv_sem=recv,
            device_id=device, device_id_type=mesh_ids,
        )
        made.start()
        return made

    order = [(d, q) for d in list(range(1, rows)) + [0] for q in range(pieces)]
    near_copies, far_copies = {}, {}
    for d, q in order:
        span = pl.ds(q * size, size)
        near_copies[d, q] = copy(
            total.at[row_at[d], 1 - core, span], near.at[d, span],
            near_send.at[d, q], near_recv.at[d, q], {"grp": partner},
        )
    for d, q in order:
        near_copies[d, q].wait()
        if d == 0:
            continue
        span = pl.ds(q * size, size)
        mid[d - 1, span] = total[row_at[d], core, span] + near[d, span]
        far_copies[d, q] = copy(
            mid.at[d - 1, span], far.at[d - 1, span],
            far_send.at[d - 1, q], far_recv.at[d - 1, q], {"grp": 2 * row_at[d] + core},
        )
    score_copies = [
        copy(
            found.at[cls_at[d]], board.at[cls],
            score_send.at[d], score_recv.at[d], {"cls": cls_at[d]},
        )
        for d in range(1, owners)
    ]
    for q in range(pieces):
        for d in range(1, rows):
            far_copies[d, q].wait()
        for n in range(q * size, (q + 1) * size):
            share = total[row, core, n] + near[0, n]
            for d in range(1, rows):
                share = share + far[d - 1, n]
            finish_class(side, bins, share, contrast, out, n)
    for made in score_copies:
        made.wait()
    board[cls] = found[cls]
    home[...] = board[...]


def close(total, found, contrast, groups, owners):
    class_local, height, side = total.shape
    rows, per = groups // 2, class_local // groups
    pieces = math.gcd(per, 2)
    dma = pltpu.SemaphoreType.DMA
    vmem = pl.BlockSpec(memory_space=pltpu.VMEM)
    return pl.pallas_call(
        functools.partial(close_kernel, side, contrast.shape[0], groups, owners),
        in_specs=[vmem] * 3,
        out_specs=[vmem] * 2,
        out_shape=[
            jax.ShapeDtypeStruct((per, 2, side, side), f32),
            jax.ShapeDtypeStruct(found.shape, f32),
        ],
        scratch_shapes=[
            pltpu.VMEM((rows, per, height, side), f32),
            pltpu.VMEM((max(1, rows - 1), per, height, side), f32),
            pltpu.VMEM((max(1, rows - 1), per, height, side), f32),
            pltpu.VMEM(found.shape, f32),
            dma((rows, pieces)),
            dma((rows, pieces)),
            dma((max(1, rows - 1), pieces)),
            dma((max(1, rows - 1), pieces)),
            dma((owners,)),
            dma((owners,)),
        ],
        compiler_params=pltpu.CompilerParams(
            collective_id=0, has_side_effects=True, vmem_limit_bytes=VMEM_BYTES
        ),
        cost_estimate=pl.CostEstimate(
            flops=per * 20_000_000, bytes_accessed=8_000_000, transcendentals=0
        ),
        name="close",
    )(total.reshape(rows, 2, per, height, side), found, contrast)


def body(
    particles, references, class_of, rotation_bin, shift_best, defocus_bin, shift_list, defocus
):
    side = particles.shape[-1]
    part_rows = particles.shape[0]
    class_local = references.shape[0]
    shifts = shift_list.shape[0]
    owners = lax.axis_size("cls")
    capacity = max(2, 2 * part_rows // owners)
    chunks = math.gcd(capacity, 4)
    slots = capacity // chunks
    slot_total = owners * capacity

    owner_of = class_of // class_local
    rows = jnp.arange(part_rows)
    before = (rows[:, None] > rows[None, :]) & (owner_of[:, None] == owner_of[None, :])
    rank = jnp.sum(before.astype(jnp.int32), axis=1)
    target = owner_of * capacity + rank
    hit = target[None, :] == jnp.arange(slot_total, dtype=jnp.int32)[:, None]
    facts = jnp.stack(
        [class_of % class_local, defocus_bin, shift_best, rotation_bin, jnp.ones_like(class_of)]
    )
    facts = jnp.sum(jnp.where(hit[None], facts[:, None, :], 0), axis=2).astype(f32)
    facts = facts.reshape(5, owners, capacity).transpose(1, 0, 2)
    facts = lax.all_to_all(facts, "cls", split_axis=0, concat_axis=0, tiled=True)
    source = jnp.sum(jnp.where(hit, rows.astype(jnp.int32)[None, :], 0), axis=1)
    send = particles[source].reshape(owners, capacity * side, side)

    right, left = dft_tables(side)
    contrast = contrast_half(defocus, side)
    phase, score_right, score_left = shift_tables(shift_list, side)
    tables = (contrast, phase, split_table(right), split_table(left), split_table(score_right), score_left)

    facts = facts.astype(jnp.int32).reshape(owners, 5, chunks, slots).transpose(1, 2, 0, 3)
    facts = facts.reshape(5, slot_total)
    count = jnp.arange(slot_total, dtype=jnp.int32)
    alike = (facts[0][:, None] == facts[0][None, :]) & (facts[4][None, :] > 0)
    alike = alike & (count[None, :] < count[:, None])
    earlier = jnp.max(jnp.where(alike, count[None, :] + 1, 0), axis=1)
    of_class = facts[0][None, :] == jnp.arange(class_local, dtype=jnp.int32)[:, None]
    last = jnp.max(jnp.where(of_class & (facts[4][None, :] > 0), count[None, :] + 1, 0), axis=1)
    info = jnp.concatenate([facts, earlier[None]], axis=0)

    found, total = gather_terms(send, info, last, references, tables, chunks)
    found = found.transpose(1, 0, 2, 3).reshape(owners, capacity, -1)
    fresh, home = close(total, found, contrast, lax.axis_size("grp"), owners)
    return home.reshape(slot_total, -1)[target][:, :shifts], fresh


def solution(mesh):
    return jax.shard_map(
        body,
        mesh=mesh,
        in_specs=(
            P(("grp", "cls"), None, None),
            P("cls", None, None, None),
            P(("grp", "cls")),
            P(("grp", "cls")),
            P(("grp", "cls")),
            P(("grp", "cls")),
            P(),
            P(),
        ),
        out_specs=(P(("grp", "cls"), None), P(("cls", "grp"), None, None, None)),
        check_vma=False,
    )
```

```python
import functools
import math

import jax
import jax.numpy as jnp
import ml_dtypes
import numpy as np
from jax import lax
from jax.experimental import pallas as pl
from jax.experimental.pallas import tpu as pltpu
from jax.sharding import PartitionSpec as P

f32, bf16 = jnp.float32, jnp.bfloat16
HALF = 72
GROUP = 8
AHEAD = 3
VMEM_BYTES = 56 * 1024 * 1024


def split(x):
    high = x.astype(bf16)
    return high, (x - high.astype(f32)).astype(bf16)


def split_table(x):
    high = lax.reduce_precision(x, 8, 7)
    return high.astype(bf16), lax.reduce_precision(x - high, 8, 7).astype(bf16)


def dot(a, b):
    return jnp.dot(a, b, preferred_element_type=f32)


def dot3(a, b):
    return dot(a[0], b[0]) + (dot(a[1], b[0]) + dot(a[0], b[1]))


def circle(turns, side):
    angles = (turns % side).astype(f32) * (2.0 * math.pi / side)
    return jnp.cos(angles), jnp.sin(angles)


def dft_tables(side):
    pixel = np.arange(side)
    live = (np.arange(HALF) <= side // 2)[:, None]
    right, left = [], []
    for place in (pixel, side - 1 - pixel):
        angles = (pixel[:, None] * place[None, :] % side) * (2.0 * math.pi / side)
        c, s = np.cos(angles) / math.sqrt(side), np.sin(angles) / math.sqrt(side)
        right.append(np.concatenate([c.T, s.T], axis=1))
        c, s = c[:HALF] * live, s[:HALF] * live
        left.append(np.block([[c, -s], [-s, -c]]))

    def halves(x):
        x = np.stack(x)
        high = x.astype(ml_dtypes.bfloat16)
        low = (x - high.astype(np.float64)).astype(ml_dtypes.bfloat16)
        return jnp.asarray(high), jnp.asarray(low)

    return halves(right), halves(left)


def contrast_half(defocus, side):
    pixel = jnp.arange(side, dtype=jnp.int32)
    signed = jnp.where(pixel < side // 2, pixel, pixel - side).astype(f32)
    rows = signed[:HALF]
    radius = (rows[:, None] * rows[:, None] + signed[None, :] * signed[None, :]) / float(
        (side // 2) ** 2
    )
    phases = defocus[:, None, None] * radius[None]
    return -(0.995 * jnp.sin(phases) + 0.1 * jnp.cos(phases))


def shift_tables(shift_list, side):
    row_cos, row_sin = circle(
        shift_list[:, 0][:, None] * jnp.arange(HALF, dtype=jnp.int32)[None, :], side
    )
    col_cos, col_sin = circle(
        shift_list[:, 1][:, None] * jnp.arange(side, dtype=jnp.int32)[None, :], side
    )
    row_table = jnp.concatenate([row_cos.T, row_sin.T], axis=0)
    col_table = jnp.stack([col_cos, col_sin], axis=1)
    score_right = jnp.concatenate([col_cos.T, col_sin.T], axis=1)
    row = jnp.arange(HALF)
    times = jnp.where(
        (row == 0) | (row == side // 2), 1.0, jnp.where(row < side // 2, 2.0, 0.0)
    ).astype(f32)[:, None] / side
    uc, us = row_cos.T * times, row_sin.T * times
    score_left = jnp.concatenate(
        [jnp.concatenate([uc, -us], axis=1), jnp.concatenate([-us, -uc], axis=1)], axis=0
    )
    return row_table, col_table, score_right, score_left


def mirror_pick(rows, cols, side, offset):
    i = lax.broadcasted_iota(jnp.int32, (rows, cols), 0)
    j = lax.broadcasted_iota(jnp.int32, (rows, cols), 1)
    return jnp.where((i + j) % side == offset, 1.0, 0.0).astype(bf16)


def mirrored(x, row_pick, col_pick):
    total = None
    for piece in split(x):
        turned = dot(dot(row_pick, piece).astype(bf16), col_pick)
        total = turned if total is None else total + turned
    return total


def gather_kernel(
    side, owners, chunks, facts, send, references, contrast, row_table, col_table,
    right_hi, right_lo, left_hi, left_lo, sr_hi, sr_lo, score_left, scores, total,
    got, held_refs, refs, running, fact_board, info, newest, last, earlier,
    send_sem, recv_sem, fact_send, fact_recv, local_sem,
):
    mesh_ids = pl.DeviceIdType.MESH
    cls = lax.axis_index("cls")
    slots = scores.shape[2]
    span = slots * side
    classes = refs.shape[0]

    local_copies = [
        pltpu.make_async_copy(references, held_refs, local_sem.at[0]),
        pltpu.make_async_copy(send.at[cls], got.at[cls], local_sem.at[1]),
    ]

    def copy(r, d):
        to = lax.rem(cls + d, owners)
        rows = pl.ds(pl.multiple_of(r * span, side), span)
        return pltpu.make_async_remote_copy(
            src_ref=send.at[to, rows], dst_ref=got.at[cls, rows],
            send_sem=send_sem.at[r, d], recv_sem=recv_sem.at[r, d],
            device_id={"cls": to}, device_id_type=mesh_ids,
        )

    barrier = pltpu.get_barrier_semaphore()
    for d in range(1, owners):
        pl.semaphore_signal(
            barrier, inc=1, device_id={"cls": lax.rem(cls + d, owners)}, device_id_type=mesh_ids
        )
    for made in local_copies:
        made.start()
    pl.semaphore_wait(barrier, owners - 1)
    fact_copies = []
    for d in range(1, owners):
        to = lax.rem(cls + d, owners)
        made = pltpu.make_async_remote_copy(
            src_ref=facts.at[to], dst_ref=fact_board.at[cls],
            send_sem=fact_send.at[d], recv_sem=fact_recv.at[d],
            device_id={"cls": to}, device_id_type=mesh_ids,
        )
        made.start()
        fact_copies.append(made)
    for r in range(min(AHEAD, chunks)):
        for d in range(1, owners):
            copy(r, d).start()

    running[0] = jnp.zeros(running.shape[1:], f32)
    for made in local_copies:
        made.wait()
    row_pick = mirror_pick(HALF, side, side, 0)
    col_pick = mirror_pick(side, side, side, 0)
    live_row = lax.broadcasted_iota(jnp.int32, (HALF, side), 0) <= side // 2
    at_once = math.gcd(classes, 4)

    def halve(step, carry):
        for n in range(at_once):
            for part, sign in ((0, 1.0), (1, -1.0)):
                x = held_refs[step * at_once + n, part]
                both = 0.5 * (x[:HALF] + sign * mirrored(x, row_pick, col_pick))
                refs[step * at_once + n, part] = jnp.where(live_row, both, 0.0)
        return carry

    lax.fori_loop(0, classes // at_once, halve, 0)

    fact_board[cls] = facts[cls]
    for made in fact_copies:
        made.wait()
    to_scalars = pltpu.make_async_copy(fact_board, info, local_sem.at[2])
    to_scalars.start()
    to_scalars.wait()
    lanes = lax.broadcasted_iota(jnp.int32, (8, side), 1)

    def chain(n, seen):
        source, at = n // slots % owners, n // (slots * owners) * slots + n % slots
        key = info[source, 0, at] + (1 - info[source, 4, at]) * classes
        mine = lanes == key
        earlier[n] = jnp.max(jnp.where(mine, seen, 0))
        return jnp.where(mine, n + 1, seen)

    newest[...] = lax.fori_loop(
        0, owners * slots * chunks, chain, jnp.zeros((8, side), jnp.int32)
    )
    to_scalars = pltpu.make_async_copy(newest, last, local_sem.at[3])
    to_scalars.start()
    to_scalars.wait()

    lane = lax.broadcasted_iota(jnp.int32, (8, side), 1)
    tail_row = lax.broadcasted_iota(jnp.int32, (8, side), 0)
    block = math.gcd(owners, max(1, GROUP // slots))

    shift_lane = lax.broadcasted_iota(jnp.int32, row_table.shape, 1)

    def particle(source, at, image):
        local, bin_at, shift = info[source, 0, at], info[source, 1, at], info[source, 2, at]
        turns, live = info[source, 3, at], info[source, 4, at].astype(f32)
        image = jnp.where(turns % 2 == 1, image.T, image)
        right_at = (turns >= 2).astype(jnp.int32)
        left_at = ((turns == 1) | (turns == 2)).astype(jnp.int32)
        halfway = dot3(split(image), (right_hi[right_at], right_lo[right_at]))
        halfway = jnp.concatenate([halfway[:, :side], halfway[:, side:]], axis=0)
        spec = dot3((left_hi[left_at], left_lo[left_at]), split(halfway))
        gain = contrast[bin_at] * live
        re, im = spec[:HALF] * gain, spec[HALF:] * gain
        ref_re, ref_im = refs[local, 0], refs[local, 1]
        product = jnp.concatenate([re * ref_re + im * ref_im, im * ref_re - re * ref_im], axis=0)
        part = dot3(split(product), (sr_hi[...], sr_lo[...]))
        score = jnp.sum(part * score_left[...], axis=0, keepdims=True)
        factor = jnp.sum(jnp.where(shift_lane == shift, row_table[...], 0.0), axis=1, keepdims=True)
        col = col_table[shift]
        cos = factor[:HALF] * col[:1] - factor[HALF:] * col[1:]
        sin = factor[HALF:] * col[:1] + factor[:HALF] * col[1:]
        con_re, con_im = re * cos - im * sin, im * cos + re * sin
        tail = jnp.where((tail_row == 1) & (lane == bin_at), live, con_re[side // 2 :])
        return score, jnp.concatenate([con_re[: side // 2], tail, con_im], axis=0)

    def chunk(r, carry):
        for d in range(1, owners):
            copy(r, d).wait()

        @pl.when(r + AHEAD < chunks)
        def _():
            for d in range(1, owners):
                copy(r + AHEAD, d).start()

        def sources(step, inner):
            base = (r * owners + step * block) * slots
            found, parts = [], []
            for n in range(block * slots):
                start = pl.multiple_of(r * span + n % slots * side, side)
                score, part = particle(
                    step * block + n // slots, r * slots + n % slots,
                    got[step * block + n // slots, pl.ds(start, side)],
                )
                found.append(score)
                parts.append(part)
            for n in range(block * slots):
                running[base + n + 1] = running[earlier[base + n]] + parts[n]
            found = jnp.concatenate(found, axis=0)
            found = found + pltpu.roll(found, found.shape[1] // 2, 1)
            for n in range(block):
                scores[r, step * block + n] = found[n * slots : (n + 1) * slots]
            return inner

        return lax.fori_loop(0, owners // block, sources, carry)

    lax.fori_loop(0, chunks, chunk, 0)

    def close_class(c, carry):
        total[c] = running[last[0, c]]
        return carry

    lax.fori_loop(0, classes, close_class, 0)


def gather_terms(send, facts, references, tables, chunks):
    owners, held, side = send.shape
    slots = held // side // chunks
    class_local = references.shape[0]
    contrast, row_table, col_table, right, left, score_right, score_left = tables
    lanes = score_left.shape[1]
    vmem = pl.BlockSpec(memory_space=pltpu.VMEM)
    hbm = pl.BlockSpec(memory_space=pl.ANY)
    dma = pltpu.SemaphoreType.DMA
    return pl.pallas_call(
        functools.partial(gather_kernel, side, owners, chunks),
        in_specs=[vmem, hbm, hbm] + [vmem] * 10,
        out_specs=[vmem, vmem],
        out_shape=[
            jax.ShapeDtypeStruct((chunks, owners, slots, lanes), f32),
            jax.ShapeDtypeStruct((class_local, 2 * HALF, side), f32),
        ],
        scratch_shapes=[
            pltpu.VMEM(send.shape, f32),
            pltpu.VMEM(references.shape, f32),
            pltpu.VMEM((class_local, 2, HALF, side), f32),
            pltpu.VMEM((owners * slots * chunks + 1, 2 * HALF, side), f32),
            pltpu.VMEM(facts.shape, jnp.int32),
            pltpu.SMEM(facts.shape, jnp.int32),
            pltpu.VMEM((8, side), jnp.int32),
            pltpu.SMEM((8, side), jnp.int32),
            pltpu.SMEM((owners * slots * chunks,), jnp.int32),
            dma((chunks, owners)),
            dma((chunks, owners)),
            dma((owners,)),
            dma((owners,)),
            dma((4,)),
        ],
        compiler_params=pltpu.CompilerParams(
            collective_id=1, has_side_effects=True, vmem_limit_bytes=VMEM_BYTES
        ),
        cost_estimate=pl.CostEstimate(
            flops=owners * slots * chunks * 70_000_000, bytes_accessed=30_000_000,
            transcendentals=0,
        ),
        name="gather_terms",
    )(
        facts, send, references, contrast, row_table, col_table, *right, *left, *score_right, score_left
    )


def finish_class(side, bins, share, contrast, out, n):
    row_pick = mirror_pick(side // 2, HALF, side, side // 2)
    col_pick = mirror_pick(side, side, side, 0)
    tail_row = lax.broadcasted_iota(jnp.int32, (8, side), 0)
    middle = side // 2
    counts = share[middle + 1 : middle + 2]
    weight = jnp.ones((HALF, side), f32)
    for d in range(bins):
        weight += counts[:, d : d + 1] * (contrast[d] * contrast[d])
    live = lax.broadcasted_iota(jnp.int32, (HALF, side), 0) <= middle
    for part, sign in ((0, 1.0), (1, -1.0)):
        fresh = jnp.where(live, share[part * HALF : (part + 1) * HALF], 0.0) / weight
        other = sign * mirrored(fresh, row_pick, col_pick)
        out[n, part, :middle] = fresh[:middle]
        out[n, part, middle : middle + 8] = jnp.where(tail_row == 0, fresh[middle:], other[:8])
        out[n, part, middle + 8 :] = other[8:]


def close_kernel(
    side, bins, groups, owners, total, found, contrast, out, home,
    near, mid, far, board, near_send, near_recv, far_send, far_recv, score_send, score_recv,
):
    mesh_ids = pl.DeviceIdType.MESH
    grp, cls = lax.axis_index("grp"), lax.axis_index("cls")
    row, core = grp // 2, grp % 2
    rows = groups // 2
    pieces = near_send.shape[1]
    per = total.shape[2]
    size = per // pieces
    partner = 2 * row + (1 - core)
    row_at = [lax.rem(row + d, rows) for d in range(rows)]
    cls_at = [lax.rem(cls + d, owners) for d in range(owners)]

    barrier = pltpu.get_barrier_semaphore()
    greet = [{"grp": partner}] + [{"grp": 2 * row_at[d] + core} for d in range(1, rows)]
    greet += [{"cls": cls_at[d]} for d in range(1, owners)]
    for device in greet:
        pl.semaphore_signal(barrier, inc=1, device_id=device, device_id_type=mesh_ids)
    pl.semaphore_wait(barrier, len(greet))

    def copy(source, target, send, recv, device):
        made = pltpu.make_async_remote_copy(
            src_ref=source, dst_ref=target, send_sem=send, recv_sem=recv,
            device_id=device, device_id_type=mesh_ids,
        )
        made.start()
        return made

    order = [(d, q) for d in list(range(1, rows)) + [0] for q in range(pieces)]
    near_copies, far_copies = {}, {}
    for d, q in order:
        span = pl.ds(q * size, size)
        near_copies[d, q] = copy(
            total.at[row_at[d], 1 - core, span], near.at[d, span],
            near_send.at[d, q], near_recv.at[d, q], {"grp": partner},
        )
    for d, q in order:
        near_copies[d, q].wait()
        if d == 0:
            continue
        span = pl.ds(q * size, size)
        mid[d - 1, span] = total[row_at[d], core, span] + near[d, span]
        far_copies[d, q] = copy(
            mid.at[d - 1, span], far.at[d - 1, span],
            far_send.at[d - 1, q], far_recv.at[d - 1, q], {"grp": 2 * row_at[d] + core},
        )
    score_copies = [
        copy(
            found.at[cls_at[d]], board.at[cls],
            score_send.at[d], score_recv.at[d], {"cls": cls_at[d]},
        )
        for d in range(1, owners)
    ]
    for q in range(pieces):
        for d in range(1, rows):
            far_copies[d, q].wait()
        for n in range(q * size, (q + 1) * size):
            share = total[row, core, n] + near[0, n]
            for d in range(1, rows):
                share = share + far[d - 1, n]
            finish_class(side, bins, share, contrast, out, n)
    for made in score_copies:
        made.wait()
    board[cls] = found[cls]
    home[...] = board[...]


def close(total, found, contrast, groups, owners):
    class_local, height, side = total.shape
    rows, per = groups // 2, class_local // groups
    pieces = math.gcd(per, 2)
    dma = pltpu.SemaphoreType.DMA
    vmem = pl.BlockSpec(memory_space=pltpu.VMEM)
    return pl.pallas_call(
        functools.partial(close_kernel, side, contrast.shape[0], groups, owners),
        in_specs=[vmem] * 3,
        out_specs=[vmem] * 2,
        out_shape=[
            jax.ShapeDtypeStruct((per, 2, side, side), f32),
            jax.ShapeDtypeStruct(found.shape, f32),
        ],
        scratch_shapes=[
            pltpu.VMEM((rows, per, height, side), f32),
            pltpu.VMEM((max(1, rows - 1), per, height, side), f32),
            pltpu.VMEM((max(1, rows - 1), per, height, side), f32),
            pltpu.VMEM(found.shape, f32),
            dma((rows, pieces)),
            dma((rows, pieces)),
            dma((max(1, rows - 1), pieces)),
            dma((max(1, rows - 1), pieces)),
            dma((owners,)),
            dma((owners,)),
        ],
        compiler_params=pltpu.CompilerParams(
            collective_id=0, has_side_effects=True, vmem_limit_bytes=VMEM_BYTES
        ),
        cost_estimate=pl.CostEstimate(
            flops=per * 20_000_000, bytes_accessed=8_000_000, transcendentals=0
        ),
        name="close",
    )(total.reshape(rows, 2, per, height, side), found, contrast)


def body(
    particles, references, class_of, rotation_bin, shift_best, defocus_bin, shift_list, defocus
):
    side = particles.shape[-1]
    part_rows = particles.shape[0]
    class_local = references.shape[0]
    shifts = shift_list.shape[0]
    owners = lax.axis_size("cls")
    capacity = max(2, 2 * part_rows // owners)
    chunks = math.gcd(capacity, 8)
    slots = capacity // chunks
    slot_total = owners * capacity

    owner_of = class_of // class_local
    rows = jnp.arange(part_rows)
    before = (rows[:, None] > rows[None, :]) & (owner_of[:, None] == owner_of[None, :])
    rank = jnp.sum(before.astype(jnp.int32), axis=1)
    target = owner_of * capacity + rank
    hit = target[None, :] == jnp.arange(slot_total, dtype=jnp.int32)[:, None]
    facts = jnp.stack(
        [class_of % class_local, defocus_bin, shift_best, rotation_bin, jnp.ones_like(class_of)]
    )
    facts = jnp.sum(jnp.where(hit[None], facts[:, None, :], 0), axis=2)
    facts = facts.reshape(5, owners, capacity).transpose(1, 0, 2)
    facts = jnp.pad(facts, ((0, 0), (0, 3), (0, side - capacity)))
    source = jnp.sum(jnp.where(hit, rows.astype(jnp.int32)[None, :], 0), axis=1)
    send = particles[source].reshape(owners, capacity * side, side)

    right, left = dft_tables(side)
    contrast = contrast_half(defocus, side)
    row_table, col_table, score_right, score_left = shift_tables(shift_list, side)
    tables = (contrast, row_table, col_table, right, left, split_table(score_right), score_left)

    found, total = gather_terms(send, facts, references, tables, chunks)
    found = found.transpose(1, 0, 2, 3).reshape(owners, capacity, -1)
    fresh, home = close(total, found, contrast, lax.axis_size("grp"), owners)
    return home.reshape(slot_total, -1)[target][:, :shifts], fresh


def solution(mesh):
    return jax.shard_map(
        body,
        mesh=mesh,
        in_specs=(
            P(("grp", "cls"), None, None),
            P("cls", None, None, None),
            P(("grp", "cls")),
            P(("grp", "cls")),
            P(("grp", "cls")),
            P(("grp", "cls")),
            P(),
            P(),
        ),
        out_specs=(P(("grp", "cls"), None), P(("cls", "grp"), None, None, None)),
        check_vma=False,
    )
```

```python
import functools
import math

import jax
import jax.numpy as jnp
import ml_dtypes
import numpy as np
from jax import lax
from jax.experimental import pallas as pl
from jax.experimental.pallas import tpu as pltpu
from jax.sharding import PartitionSpec as P

f32, bf16 = jnp.float32, jnp.bfloat16
HALF = 72
GROUP = 8
AHEAD = 5
VMEM_BYTES = 56 * 1024 * 1024


def split(x):
    high = x.astype(bf16)
    return high, (x - high.astype(f32)).astype(bf16)


def split_table(x):
    high = lax.reduce_precision(x, 8, 7)
    return high.astype(bf16), lax.reduce_precision(x - high, 8, 7).astype(bf16)


def dot(a, b):
    return jnp.dot(a, b, preferred_element_type=f32)


def dot3(a, b):
    return dot(a[0], b[0]) + (dot(a[1], b[0]) + dot(a[0], b[1]))


def circle(turns, side):
    angles = (turns % side).astype(f32) * (2.0 * math.pi / side)
    return jnp.cos(angles), jnp.sin(angles)


def dft_tables(side):
    pixel = np.arange(side)
    live = (np.arange(HALF) <= side // 2)[:, None]
    right, left = [], []
    for place in (pixel, side - 1 - pixel):
        angles = (pixel[:, None] * place[None, :] % side) * (2.0 * math.pi / side)
        c, s = np.cos(angles) / math.sqrt(side), np.sin(angles) / math.sqrt(side)
        right.append(np.concatenate([c.T, s.T], axis=1))
        c, s = c[:HALF] * live, s[:HALF] * live
        left.append(np.block([[c, -s], [-s, -c]]))

    def halves(x):
        x = np.stack(x)
        high = x.astype(ml_dtypes.bfloat16)
        low = (x - high.astype(np.float64)).astype(ml_dtypes.bfloat16)
        return jnp.asarray(high), jnp.asarray(low)

    return halves(right), halves(left)


def contrast_of(defocus, radius):
    phases = defocus * radius
    quarter = jnp.floor(phases * (2.0 / math.pi) + 0.5)
    x = ((phases - quarter * 1.5703125) - quarter * 4.837512969970703125e-4)
    x = x - quarter * 7.54978995489188216e-8
    z = x * x
    sin = x + x * z * ((-1.9515295891e-4 * z + 8.3321608736e-3) * z - 1.6666654611e-1)
    cos = (1.0 - 0.5 * z) + z * z * (
        (2.443315711809948e-5 * z - 1.388731625493765e-3) * z + 4.166664568298827e-2
    )
    turn = quarter - 4.0 * jnp.floor(quarter * 0.25)
    odd = (turn == 1.0) | (turn == 3.0)
    sin, cos = jnp.where(odd, cos, sin), jnp.where(odd, sin, cos)
    sin = jnp.where(turn >= 2.0, -sin, sin)
    cos = jnp.where((turn == 1.0) | (turn == 2.0), -cos, cos)
    return -(0.995 * sin + 0.1 * cos)


def shift_tables(shift_list, side):
    row_cos, row_sin = circle(
        shift_list[:, 0][:, None] * jnp.arange(HALF, dtype=jnp.int32)[None, :], side
    )
    col_cos, col_sin = circle(
        shift_list[:, 1][:, None] * jnp.arange(side, dtype=jnp.int32)[None, :], side
    )
    row_table = jnp.concatenate([row_cos.T, row_sin.T], axis=0)
    col_table = jnp.stack([col_cos, col_sin], axis=1)
    score_right = jnp.concatenate([col_cos.T, col_sin.T], axis=1)
    row = jnp.arange(HALF)
    times = jnp.where(
        (row == 0) | (row == side // 2), 1.0, jnp.where(row < side // 2, 2.0, 0.0)
    ).astype(f32)[:, None] / side
    uc, us = row_cos.T * times, row_sin.T * times
    score_left = jnp.concatenate(
        [jnp.concatenate([uc, -us], axis=1), jnp.concatenate([-us, -uc], axis=1)], axis=0
    )
    return row_table, col_table, score_right, score_left


def mirror_pick(rows, cols, side, offset):
    i = lax.broadcasted_iota(jnp.int32, (rows, cols), 0)
    j = lax.broadcasted_iota(jnp.int32, (rows, cols), 1)
    return jnp.where((i + j) % side == offset, 1.0, 0.0).astype(bf16)


def mirrored(x, row_pick, col_pick):
    total = None
    for piece in split(x):
        turned = dot(dot(row_pick, piece).astype(bf16), col_pick)
        total = turned if total is None else total + turned
    return total


def gather_kernel(
    side, owners, chunks, defocus, facts, send, references, row_table, col_table,
    right_hi, right_lo, left_hi, left_lo, sr_hi, sr_lo, score_left, scores, total, contrast,
    got, held_refs, refs, running, fact_board, info, newest, last, earlier,
    send_sem, recv_sem, fact_send, fact_recv, local_sem,
):
    mesh_ids = pl.DeviceIdType.MESH
    cls = lax.axis_index("cls")
    slots = scores.shape[2]
    span = slots * side
    classes = refs.shape[0]

    local_copies = [
        pltpu.make_async_copy(references, held_refs, local_sem.at[0]),
        pltpu.make_async_copy(send.at[cls], got.at[cls], local_sem.at[1]),
    ]

    def copy(r, d):
        to = lax.rem(cls + d, owners)
        rows = pl.ds(pl.multiple_of(r * span, side), span)
        return pltpu.make_async_remote_copy(
            src_ref=send.at[to, rows], dst_ref=got.at[cls, rows],
            send_sem=send_sem.at[r, d], recv_sem=recv_sem.at[r, d],
            device_id={"cls": to}, device_id_type=mesh_ids,
        )

    barrier = pltpu.get_barrier_semaphore()
    for d in range(1, owners):
        pl.semaphore_signal(
            barrier, inc=1, device_id={"cls": lax.rem(cls + d, owners)}, device_id_type=mesh_ids
        )
    for made in local_copies:
        made.start()
    pl.semaphore_wait(barrier, owners - 1)
    fact_copies = []
    for d in range(1, owners):
        to = lax.rem(cls + d, owners)
        made = pltpu.make_async_remote_copy(
            src_ref=facts.at[to], dst_ref=fact_board.at[cls],
            send_sem=fact_send.at[d], recv_sem=fact_recv.at[d],
            device_id={"cls": to}, device_id_type=mesh_ids,
        )
        made.start()
        fact_copies.append(made)
    for r in range(min(AHEAD, chunks)):
        for d in range(1, owners):
            copy(r, d).start()

    running[0] = jnp.zeros(running.shape[1:], f32)
    u = lax.broadcasted_iota(jnp.int32, (HALF, side), 0)
    v = lax.broadcasted_iota(jnp.int32, (HALF, side), 1)
    u = jnp.where(u < side // 2, u, u - side).astype(f32)
    v = jnp.where(v < side // 2, v, v - side).astype(f32)
    radius = (u * u + v * v) / float((side // 2) ** 2)

    def fill(d, carry):
        contrast[d] = contrast_of(defocus[d], radius)
        return carry

    lax.fori_loop(0, contrast.shape[0], fill, 0)
    for made in local_copies:
        made.wait()
    row_pick = mirror_pick(HALF, side, side, 0)
    col_pick = mirror_pick(side, side, side, 0)
    live_row = lax.broadcasted_iota(jnp.int32, (HALF, side), 0) <= side // 2
    at_once = math.gcd(classes, 4)

    def halve(step, carry):
        for n in range(at_once):
            for part, sign in ((0, 1.0), (1, -1.0)):
                x = held_refs[step * at_once + n, part]
                both = 0.5 * (x[:HALF] + sign * mirrored(x, row_pick, col_pick))
                refs[step * at_once + n, part] = jnp.where(live_row, both, 0.0)
        return carry

    lax.fori_loop(0, classes // at_once, halve, 0)

    fact_board[cls] = facts[cls]
    for made in fact_copies:
        made.wait()
    to_scalars = pltpu.make_async_copy(fact_board, info, local_sem.at[2])
    to_scalars.start()
    to_scalars.wait()
    lanes = lax.broadcasted_iota(jnp.int32, (8, side), 1)

    def chain(n, seen):
        source, at = n // slots % owners, n // (slots * owners) * slots + n % slots
        key = info[source, 0, at] + (1 - info[source, 4, at]) * classes
        mine = lanes == key
        earlier[n] = jnp.max(jnp.where(mine, seen, 0))
        return jnp.where(mine, n + 1, seen)

    newest[...] = lax.fori_loop(
        0, owners * slots * chunks, chain, jnp.zeros((8, side), jnp.int32)
    )
    to_scalars = pltpu.make_async_copy(newest, last, local_sem.at[3])
    to_scalars.start()
    to_scalars.wait()

    lane = lax.broadcasted_iota(jnp.int32, (8, side), 1)
    tail_row = lax.broadcasted_iota(jnp.int32, (8, side), 0)
    block = math.gcd(owners, max(1, GROUP // slots))

    shift_lane = lax.broadcasted_iota(jnp.int32, row_table.shape, 1)

    def particle(source, at, image):
        local, bin_at, shift = info[source, 0, at], info[source, 1, at], info[source, 2, at]
        turns, live = info[source, 3, at], info[source, 4, at].astype(f32)
        image = jnp.where(turns % 2 == 1, image.T, image)
        right_at = (turns >= 2).astype(jnp.int32)
        left_at = ((turns == 1) | (turns == 2)).astype(jnp.int32)
        halfway = dot3(split(image), (right_hi[right_at], right_lo[right_at]))
        halfway = jnp.concatenate([halfway[:, :side], halfway[:, side:]], axis=0)
        spec = dot3((left_hi[left_at], left_lo[left_at]), split(halfway))
        gain = contrast[bin_at] * live
        re, im = spec[:HALF] * gain, spec[HALF:] * gain
        ref_re, ref_im = refs[local, 0], refs[local, 1]
        product = jnp.concatenate([re * ref_re + im * ref_im, im * ref_re - re * ref_im], axis=0)
        part = dot3(split(product), (sr_hi[...], sr_lo[...]))
        score = jnp.sum(part * score_left[...], axis=0, keepdims=True)
        factor = jnp.sum(jnp.where(shift_lane == shift, row_table[...], 0.0), axis=1, keepdims=True)
        col = col_table[shift]
        cos = factor[:HALF] * col[:1] - factor[HALF:] * col[1:]
        sin = factor[HALF:] * col[:1] + factor[:HALF] * col[1:]
        con_re, con_im = re * cos - im * sin, im * cos + re * sin
        tail = jnp.where((tail_row == 1) & (lane == bin_at), live, con_re[side // 2 :])
        return score, jnp.concatenate([con_re[: side // 2], tail, con_im], axis=0)

    def chunk(r, carry):
        for d in range(1, owners):
            copy(r, d).wait()

        @pl.when(r + AHEAD < chunks)
        def _():
            for d in range(1, owners):
                copy(r + AHEAD, d).start()

        def sources(step, inner):
            base = (r * owners + step * block) * slots
            found, parts = [], []
            for n in range(block * slots):
                start = pl.multiple_of(r * span + n % slots * side, side)
                score, part = particle(
                    step * block + n // slots, r * slots + n % slots,
                    got[step * block + n // slots, pl.ds(start, side)],
                )
                found.append(score)
                parts.append(part)
            for n in range(block * slots):
                running[base + n + 1] = running[earlier[base + n]] + parts[n]
            found = jnp.concatenate(found, axis=0)
            found = found + pltpu.roll(found, found.shape[1] // 2, 1)
            for n in range(block):
                scores[r, step * block + n] = found[n * slots : (n + 1) * slots]
            return inner

        return lax.fori_loop(0, owners // block, sources, carry)

    lax.fori_loop(0, chunks, chunk, 0)

    def close_class(c, carry):
        total[c] = running[last[0, c]]
        return carry

    lax.fori_loop(0, classes, close_class, 0)


def gather_terms(send, facts, references, defocus, tables, chunks):
    owners, held, side = send.shape
    slots = held // side // chunks
    class_local = references.shape[0]
    row_table, col_table, right, left, score_right, score_left = tables
    lanes = score_left.shape[1]
    vmem = pl.BlockSpec(memory_space=pltpu.VMEM)
    hbm = pl.BlockSpec(memory_space=pl.ANY)
    smem = pl.BlockSpec(memory_space=pltpu.SMEM)
    dma = pltpu.SemaphoreType.DMA
    return pl.pallas_call(
        functools.partial(gather_kernel, side, owners, chunks),
        in_specs=[smem, vmem, hbm, hbm] + [vmem] * 9,
        out_specs=[vmem] * 3,
        out_shape=[
            jax.ShapeDtypeStruct((chunks, owners, slots, lanes), f32),
            jax.ShapeDtypeStruct((class_local, 2 * HALF, side), f32),
            jax.ShapeDtypeStruct((defocus.shape[0], HALF, side), f32),
        ],
        scratch_shapes=[
            pltpu.VMEM(send.shape, f32),
            pltpu.VMEM(references.shape, f32),
            pltpu.VMEM((class_local, 2, HALF, side), f32),
            pltpu.VMEM((owners * slots * chunks + 1, 2 * HALF, side), f32),
            pltpu.VMEM(facts.shape, jnp.int32),
            pltpu.SMEM(facts.shape, jnp.int32),
            pltpu.VMEM((8, side), jnp.int32),
            pltpu.SMEM((8, side), jnp.int32),
            pltpu.SMEM((owners * slots * chunks,), jnp.int32),
            dma((chunks, owners)),
            dma((chunks, owners)),
            dma((owners,)),
            dma((owners,)),
            dma((4,)),
        ],
        compiler_params=pltpu.CompilerParams(
            collective_id=1, has_side_effects=True, vmem_limit_bytes=VMEM_BYTES
        ),
        cost_estimate=pl.CostEstimate(
            flops=owners * slots * chunks * 70_000_000, bytes_accessed=30_000_000,
            transcendentals=0,
        ),
        name="gather_terms",
    )(
        defocus, facts, send, references, row_table, col_table, *right, *left, *score_right, score_left
    )


def finish_class(side, bins, share, contrast, out, n):
    row_pick = mirror_pick(side // 2, HALF, side, side // 2)
    col_pick = mirror_pick(side, side, side, 0)
    tail_row = lax.broadcasted_iota(jnp.int32, (8, side), 0)
    middle = side // 2
    counts = share[middle + 1 : middle + 2]
    weight = jnp.ones((HALF, side), f32)
    for d in range(bins):
        weight += counts[:, d : d + 1] * (contrast[d] * contrast[d])
    live = lax.broadcasted_iota(jnp.int32, (HALF, side), 0) <= middle
    for part, sign in ((0, 1.0), (1, -1.0)):
        fresh = jnp.where(live, share[part * HALF : (part + 1) * HALF], 0.0) / weight
        other = sign * mirrored(fresh, row_pick, col_pick)
        out[n, part, :middle] = fresh[:middle]
        out[n, part, middle : middle + 8] = jnp.where(tail_row == 0, fresh[middle:], other[:8])
        out[n, part, middle + 8 :] = other[8:]


def close_kernel(
    side, bins, groups, owners, owner_of, rank, total, found, contrast, out, home,
    near, mid, far, board, near_send, near_recv, far_send, far_recv, score_send, score_recv,
):
    mesh_ids = pl.DeviceIdType.MESH
    grp, cls = lax.axis_index("grp"), lax.axis_index("cls")
    row, core = grp // 2, grp % 2
    rows = groups // 2
    pieces = near_send.shape[1]
    per = total.shape[2]
    size = per // pieces
    partner = 2 * row + (1 - core)
    row_at = [lax.rem(row + d, rows) for d in range(rows)]
    cls_at = [lax.rem(cls + d, owners) for d in range(owners)]

    barrier = pltpu.get_barrier_semaphore()
    greet = [{"grp": partner}] + [{"grp": 2 * row_at[d] + core} for d in range(1, rows)]
    greet += [{"cls": cls_at[d]} for d in range(1, owners)]
    for device in greet:
        pl.semaphore_signal(barrier, inc=1, device_id=device, device_id_type=mesh_ids)
    pl.semaphore_wait(barrier, len(greet))

    def copy(source, target, send, recv, device):
        made = pltpu.make_async_remote_copy(
            src_ref=source, dst_ref=target, send_sem=send, recv_sem=recv,
            device_id=device, device_id_type=mesh_ids,
        )
        made.start()
        return made

    order = [(d, q) for d in list(range(1, rows)) + [0] for q in range(pieces)]
    near_copies, far_copies = {}, {}
    for d, q in order:
        span = pl.ds(q * size, size)
        near_copies[d, q] = copy(
            total.at[row_at[d], 1 - core, span], near.at[d, span],
            near_send.at[d, q], near_recv.at[d, q], {"grp": partner},
        )
    for d, q in order:
        near_copies[d, q].wait()
        if d == 0:
            continue
        span = pl.ds(q * size, size)
        mid[d - 1, span] = total[row_at[d], core, span] + near[d, span]
        far_copies[d, q] = copy(
            mid.at[d - 1, span], far.at[d - 1, span],
            far_send.at[d - 1, q], far_recv.at[d - 1, q], {"grp": 2 * row_at[d] + core},
        )
    score_copies = [
        copy(
            found.at[cls_at[d]], board.at[cls],
            score_send.at[d], score_recv.at[d], {"cls": cls_at[d]},
        )
        for d in range(1, owners)
    ]
    for q in range(pieces):
        for d in range(1, rows):
            far_copies[d, q].wait()
        for n in range(q * size, (q + 1) * size):
            share = total[row, core, n] + near[0, n]
            for d in range(1, rows):
                share = share + far[d - 1, n]
            finish_class(side, bins, share, contrast, out, n)
    for made in score_copies:
        made.wait()
    board[cls] = found[cls]
    for n in range(home.shape[0]):
        home[n : n + 1] = board[owner_of[n], pl.ds(rank[n], 1)][:, : home.shape[1]]


def close(owner_of, rank, total, found, contrast, groups, owners, shifts):
    class_local, height, side = total.shape
    rows, per = groups // 2, class_local // groups
    pieces = math.gcd(per, 2)
    dma = pltpu.SemaphoreType.DMA
    vmem = pl.BlockSpec(memory_space=pltpu.VMEM)
    return pl.pallas_call(
        functools.partial(close_kernel, side, contrast.shape[0], groups, owners),
        in_specs=[pl.BlockSpec(memory_space=pltpu.SMEM)] * 2 + [vmem] * 3,
        out_specs=[vmem] * 2,
        out_shape=[
            jax.ShapeDtypeStruct((per, 2, side, side), f32),
            jax.ShapeDtypeStruct((owner_of.shape[0], shifts), f32),
        ],
        scratch_shapes=[
            pltpu.VMEM((rows, per, height, side), f32),
            pltpu.VMEM((max(1, rows - 1), per, height, side), f32),
            pltpu.VMEM((max(1, rows - 1), per, height, side), f32),
            pltpu.VMEM(found.shape, f32),
            dma((rows, pieces)),
            dma((rows, pieces)),
            dma((max(1, rows - 1), pieces)),
            dma((max(1, rows - 1), pieces)),
            dma((owners,)),
            dma((owners,)),
        ],
        compiler_params=pltpu.CompilerParams(
            collective_id=0, has_side_effects=True, vmem_limit_bytes=VMEM_BYTES
        ),
        cost_estimate=pl.CostEstimate(
            flops=per * 20_000_000, bytes_accessed=8_000_000, transcendentals=0
        ),
        name="close",
    )(owner_of, rank, total.reshape(rows, 2, per, height, side), found, contrast)


def body(
    particles, references, class_of, rotation_bin, shift_best, defocus_bin, shift_list, defocus
):
    side = particles.shape[-1]
    part_rows = particles.shape[0]
    class_local = references.shape[0]
    shifts = shift_list.shape[0]
    owners = lax.axis_size("cls")
    capacity = max(2, 2 * part_rows // owners)
    chunks = math.gcd(capacity, 8)
    slots = capacity // chunks
    slot_total = owners * capacity

    owner_of = class_of // class_local
    rows = jnp.arange(part_rows)
    before = (rows[:, None] > rows[None, :]) & (owner_of[:, None] == owner_of[None, :])
    rank = jnp.sum(before.astype(jnp.int32), axis=1)
    target = owner_of * capacity + rank
    hit = target[None, :] == jnp.arange(slot_total, dtype=jnp.int32)[:, None]
    facts = jnp.stack(
        [class_of % class_local, defocus_bin, shift_best, rotation_bin, jnp.ones_like(class_of)]
    )
    facts = jnp.sum(jnp.where(hit[None], facts[:, None, :], 0), axis=2)
    facts = facts.reshape(5, owners, capacity).transpose(1, 0, 2)
    facts = jnp.pad(facts, ((0, 0), (0, 3), (0, side - capacity)))
    source = jnp.sum(jnp.where(hit, rows.astype(jnp.int32)[None, :], 0), axis=1)
    send = particles[source].reshape(owners, capacity * side, side)

    right, left = dft_tables(side)
    row_table, col_table, score_right, score_left = shift_tables(shift_list, side)
    tables = (row_table, col_table, right, left, split_table(score_right), score_left)

    found, total, contrast = gather_terms(send, facts, references, defocus, tables, chunks)
    found = found.transpose(1, 0, 2, 3).reshape(owners, capacity, -1)
    fresh, scores = close(
        owner_of, rank, total, found, contrast, lax.axis_size("grp"), owners, shifts
    )
    return scores, fresh


def solution(mesh):
    return jax.shard_map(
        body,
        mesh=mesh,
        in_specs=(
            P(("grp", "cls"), None, None),
            P("cls", None, None, None),
            P(("grp", "cls")),
            P(("grp", "cls")),
            P(("grp", "cls")),
            P(("grp", "cls")),
            P(),
            P(),
        ),
        out_specs=(P(("grp", "cls"), None), P(("cls", "grp"), None, None, None)),
        check_vma=False,
    )
```
